128 devices in a mesh: qx: 8 (over z, core), qy: 16 (over y, x).
Axes of the slice: x: 4, y: 4, z: 4, core: 2. Of those that a mesh axis runs over, the one named last changes fastest.
Arguments:
- coeffs: float32 [8, 16, 8, 16, 2, 2, 16, 128], P('qx', 'qy'), may hold values from -0.75 to 0.75
- level_phase: float32 [8, 16, 8, 16, 4, 2, 128], P('qx', 'qy'), may hold values from -3.140625 to 3.140625
- field_phase: float32 [8, 16, 8, 16, 2, 128], P('qx', 'qy'), may hold values from -3.140625 to 3.140625
Outputs:
- field: float32 [8, 16, 8, 16, 2, 2, 16, 128], P('qx', 'qy')
The draws below stay inside these ranges and needn't reach their ends.
All inputs are finite; a program needn't handle non-finite values.
Results may differ from the reference program's by a relative error of at most 0.0003.
Values sent between devices are 32-bit elements; how exact they have to be, the bound alone decides.
A program may use at most 128 MiB of HBM per device.

```python
import jax
import jax.numpy as jnp
import numpy as np
from jax import lax

CHEB = 8
RHS = 16
LEVELS = 4
N_QX = 8
N_QY = 16


def shard_levels(rng, extent, shards, least, high):
    factor_of = 1.0
    for dim, shards_of in shards:
        heights = jax.random.uniform(jax.random.fold_in(jax.random.fold_in(rng, 6), dim), (shards_of,), jnp.float32, least / len(shards), high / len(shards))
        factor_of = factor_of * jnp.repeat(jnp.exp(heights), extent[dim] // shards_of).reshape((-1,) + (1,) * (len(extent) - 1 - dim))
    return factor_of


def gaussian(own_key, extent, deviation, limit, cuts=(), held_as=jnp.bfloat16):
    result = jax.random.normal(own_key, extent, jnp.float32) * deviation
    if len(cuts) > 0:
        result = shard_levels(own_key, extent, cuts, -0.22, 0.18) * result
    return jnp.clip(result, min=-limit, max=limit).astype(held_as)


def setup_inputs(seed: int = 0) -> dict:
    streams_of = jax.random.split(jax.random.key(seed), 4)
    return {
        "coeffs": gaussian(streams_of[0], (N_QX, N_QY, N_QX, N_QY, 2, 2, RHS, 2 * CHEB * CHEB), 0.125, 0.75, ((0, 8), (1, 16)), jnp.float32),
        "level_phase": jnp.clip(jax.random.uniform(streams_of[1], (N_QX, N_QY, N_QX, N_QY, LEVELS, 2, 2 * CHEB * CHEB), jnp.float32, -3.140625, 3.140625), -3.140625, 3.140625),
        "field_phase": jnp.clip(jax.random.uniform(streams_of[2], (N_QX, N_QY, N_QX, N_QY, 2, 2 * CHEB * CHEB), jnp.float32, -3.140625, 3.140625), -3.140625, 3.140625),
    }


def point_tables(count):
    points = 0.5 - 0.5 * np.cos((2 * np.arange(count) + 1) * np.pi / (2 * count))

    def lagrange(places):
        values = np.ones((len(places), count))
        for k in range(count):
            for m in range(count):
                if m != k:
                    values[:, k] = values[:, k] * (places - points[m]) / (points[k] - points[m])
        return values

    halves = [lagrange((q + points) / 2.0) for q in range(2)]
    uniform = lagrange((np.arange(count) + 0.5) / count)
    identity = np.eye(2)
    children = np.stack([np.stack([np.kron(identity, np.kron(halves[x_half], halves[y_half])).T for y_half in range(2)]) for x_half in range(2)])
    evaluate = np.kron(identity, np.kron(uniform, uniform)).T
    return jnp.asarray(children, jnp.float32), jnp.asarray(evaluate, jnp.float32)


def rotate(values, angles):
    width = values.shape[-1] // 2
    cosine = jnp.cos(angles)
    sine = jnp.sin(angles)
    real_part = values[..., :width]
    imag_part = values[..., width:]
    return jnp.concatenate([cosine * real_part - sine * imag_part, sine * real_part + cosine * imag_part], axis=-1)


def one_level(state, angles, level, children, x_bits, y_bits):
    rotated = rotate(state, angles)
    shape = rotated.shape
    split = rotated.reshape((2,) * x_bits + (2,) * y_bits + shape[2:])
    if level == 1:
        x_axis = x_bits + y_bits + 3
    else:
        x_axis = x_bits - 1 - (level - 2)
    y_axis = x_bits + y_bits - 1 - (level - 1)
    summed = jnp.sum(split, axis=(x_axis, y_axis), keepdims=True)
    stacked = []
    for x_half in range(2):
        columns = [jnp.matmul(summed, children[x_half, y_half], precision=lax.Precision.HIGHEST) for y_half in range(2)]
        stacked.append(jnp.concatenate(columns, axis=y_axis))
    return jnp.concatenate(stacked, axis=x_axis).reshape(shape)


def reference(coeffs, level_phase, field_phase):
    x_bits = N_QX.bit_length() - 1
    y_bits = N_QY.bit_length() - 1
    children, evaluate = point_tables(CHEB)
    half_width = CHEB * CHEB
    state = coeffs
    for level in range(1, LEVELS + 1):
        angles = level_phase[:, :, :, :, level - 1].reshape(level_phase.shape[:4] + (2, 2, 1, half_width))
        state = one_level(state, angles, level, children, x_bits, y_bits)
    values = jnp.matmul(state, evaluate, precision=lax.Precision.HIGHEST)
    angles = field_phase.reshape(field_phase.shape[:5] + (2, 1, half_width))
    return rotate(values, angles)
```

```python
import jax
import jax.numpy as jnp
import numpy as np
from jax import lax
from jax.sharding import PartitionSpec as P

CHEB = 8


def point_tables(count):
    points = 0.5 - 0.5 * np.cos((2 * np.arange(count) + 1) * np.pi / (2 * count))

    def lagrange(places):
        values = np.ones((len(places), count))
        for k in range(count):
            for m in range(count):
                if m != k:
                    values[:, k] = values[:, k] * (places - points[m]) / (points[k] - points[m])
        return values

    halves = [lagrange((q + points) / 2.0) for q in range(2)]
    uniform = lagrange((np.arange(count) + 0.5) / count)
    identity = np.eye(2)
    children = np.stack(
        [
            np.stack(
                [
                    np.kron(identity, np.kron(halves[x_half], halves[y_half])).T
                    for y_half in range(2)
                ]
            )
            for x_half in range(2)
        ]
    )
    evaluate = np.kron(identity, np.kron(uniform, uniform)).T
    return (jnp.asarray(children, jnp.float32), jnp.asarray(evaluate, jnp.float32))


def rotate(values, angles):
    width = values.shape[-1] // 2
    cosine = jnp.cos(angles)
    sine = jnp.sin(angles)
    real_part = values[..., :width]
    imag_part = values[..., width:]
    return jnp.concatenate(
        [cosine * real_part - sine * imag_part, sine * real_part + cosine * imag_part], axis=-1
    )


def spread(summed, x_axis, y_axis, children):
    stacked = []
    for x_half in range(2):
        columns = [
            jnp.matmul(summed, children[x_half, y_half], precision=lax.Precision.HIGHEST)
            for y_half in range(2)
        ]
        stacked.append(jnp.concatenate(columns, axis=y_axis))
    return jnp.concatenate(stacked, axis=x_axis)


def per_device(coeffs, level_phase, field_phase):
    children, evaluate = point_tables(CHEB)
    axes = ("qx", "qy")
    half = CHEB * CHEB
    boxes_h, boxes_v = coeffs.shape[2:4]
    rhs = coeffs.shape[6]
    n = boxes_h * boxes_v
    state = coeffs.reshape(n, 2, 2, rhs, 2 * half)
    phases = level_phase.reshape(n, 4, 2, 2, 1, half)
    partial = jnp.sum(rotate(state, phases[:, 0]), axis=2)
    moved_phase = lax.all_to_all(level_phase.reshape(n, 4, 2, 2 * half)[:, 1:], axes, 0, 0, tiled=True)
    moved = lax.all_to_all(partial, axes, 0, 0, tiled=True)
    digits = (2,) * 7
    summed = moved.reshape(digits + (1, 2, rhs, 2 * half)).sum(axis=6, keepdims=True)
    state = spread(summed, 7, 6, children)
    angles = moved_phase.reshape(digits + (3, 2, 2, half))
    for level in range(2, 5):
        turn = angles[:, :, :, :, :, :, :, level - 2]
        turn = jnp.swapaxes(turn, 7, 8).reshape(digits + (2, 2, 1, half))
        x_axis, y_axis = 4 - level, 7 - level
        summed = jnp.sum(rotate(state, turn), axis=(x_axis, y_axis), keepdims=True)
        if level < 4:
            state = spread(summed, x_axis, y_axis, children)
    out = jnp.broadcast_to(jnp.swapaxes(summed, 7, 8), digits + (2, 2, rhs, 2 * half))
    got = lax.all_to_all(out.reshape(n, 2, 2, rhs, 2 * half), axes, 0, 0, tiled=True)
    x_pick = lax.axis_index("qx") >> 2 & 1
    y_pick = lax.axis_index("qy") >> 3 & 1
    matrix = lax.dynamic_index_in_dim(
        lax.dynamic_index_in_dim(children, x_pick, 0, False), y_pick, 0, False
    )
    matrix = jnp.matmul(matrix, evaluate, precision=lax.Precision.HIGHEST)
    values = jnp.matmul(got, matrix, precision=lax.Precision.HIGHEST)
    values = rotate(values, field_phase.reshape(n, 2, 2, 1, half))
    return values.reshape(coeffs.shape)


def solution(mesh):
    return jax.shard_map(
        per_device,
        mesh=mesh,
        in_specs=(
            P("qx", "qy", None, None, None, None, None, None),
            P("qx", "qy", None, None, None, None, None),
            P("qx", "qy", None, None, None, None),
        ),
        out_specs=P("qx", "qy", None, None, None, None, None, None),
        check_vma=False,
    )
```

```python
import functools

import jax
import jax.numpy as jnp
import numpy as np
from jax import lax
from jax.experimental import pallas as pl
from jax.experimental.pallas import tpu as pltpu
from jax.sharding import PartitionSpec as P

CHEB = 8
PTS = CHEB * CHEB
WIDE = 2 * PTS
MESH = pl.DeviceIdType.MESH
F32 = jnp.float32
BF16 = jnp.bfloat16


def point_tables(count):
    points = 0.5 - 0.5 * np.cos((2 * np.arange(count) + 1) * np.pi / (2 * count))

    def lagrange(places):
        values = np.ones((len(places), count))
        for k in range(count):
            for m in range(count):
                if m != k:
                    values[:, k] = values[:, k] * (places - points[m]) / (points[k] - points[m])
        return values

    halves = [lagrange((q + points) / 2.0) for q in range(2)]
    uniform = lagrange((np.arange(count) + 0.5) / count)
    identity = np.eye(2)
    children = [
        [np.kron(identity, np.kron(halves[q], halves[s])).T for s in range(2)] for q in range(2)
    ]
    evaluate = np.kron(identity, np.kron(uniform, uniform)).T
    return children, evaluate


def three_parts(matrix):
    high = matrix.astype(np.float32).astype(BF16)
    low = (matrix - high.astype(np.float64)).astype(np.float32).astype(BF16)
    return np.concatenate([high, high, low], axis=0)


def weights():
    children, evaluate = point_tables(CHEB)
    spread = three_parts(np.concatenate([children[q][s] for q in range(2) for s in range(2)], axis=1))
    last = []
    for q in range(2):
        for s in range(2):
            both = children[q][s] @ evaluate
            swapped = np.concatenate([both[:, PTS:], both[:, :PTS]], axis=1)
            last.append(three_parts(np.concatenate([both, swapped], axis=1)))
    return jnp.asarray(spread), jnp.asarray(np.stack(last))


def split_parts(value):
    high = value.astype(BF16)
    low = (value - high.astype(F32)).astype(BF16)
    return high, low


def sine_cosine(angle):
    u = angle * 0.5
    w = u * u
    s = -2.5052108e-08
    for c in (2.7557319e-06, -1.9841270e-04, 8.3333333e-03, -1.6666667e-01, 1.0):
        s = s * w + c
    s = s * u
    c_ = 2.0876757e-09
    for c in (-2.7557319e-07, 2.4801587e-05, -1.3888889e-03, 4.1666667e-02, -0.5, 1.0):
        c_ = c_ * w + c
    return 2.0 * s * c_, 1.0 - 2.0 * s * s


def swap(value):
    return pltpu.roll(value, PTS, value.ndim - 1)


def turn_tables(angle, before):
    sine, cosine = sine_cosine(angle)
    lane = lax.broadcasted_iota(jnp.int32, angle.shape, angle.ndim - 1)
    low = lane < PTS
    cos_swap, sin_swap = swap(cosine), swap(sine)
    cos = (jnp.where(low, cosine, cos_swap), jnp.where(low, cos_swap, cosine))
    if before:
        sin = (jnp.where(low, sine, -sin_swap), jnp.where(low, sin_swap, -sine))
    else:
        sin = (jnp.where(low, -sine, sin_swap), jnp.where(low, -sin_swap, sine))
    return cos, sin


def wait_for(ref, sem):
    pltpu.make_async_copy(ref, ref, sem).wait()


def exchange_kernel(
    coeffs, phases, w_ref, gz, gy,
    cbuf, lpv, cos1, sin1, sendx, recvx, send1, recv1, p1, phs, cos_t, sin_t, xs, res, s4, r1,
    load_sem, x_send, x_recv, in_send, in_recv, s1_send, s1_recv, s2_send, s2_recv, own_sem,
    ph_send, ph_recv,
):
    big_x = lax.axis_index("qx")
    big_y = lax.axis_index("qy")
    z, core = big_x // 2, big_x % 2
    y, x = big_y // 4, big_y % 4

    phase_load = pltpu.make_async_copy(phases, lpv, load_sem.at[2])
    phase_load.start()
    loads = []
    for left in range(2):
        load = pltpu.make_async_copy(coeffs.at[:, left], cbuf.at[left], load_sem.at[left])
        load.start()
        loads.append(load)

    def device(dz, dc, dy, dx):
        return ((z + dz) % 4) * 2 + (core + dc) % 2, ((y + dy) % 4) * 4 + (x + dx) % 4

    barrier = pltpu.get_barrier_semaphore()
    greeted = 0
    for dz in range(4):
        for dc in range(2):
            for dy in range(4):
                for dx in range(4):
                    if (dz, dc, dy, dx) != (0, 0, 0, 0) and 0 in (dz, dy, dx):
                        pl.semaphore_signal(
                            barrier, inc=1, device_id=device(dz, dc, dy, dx), device_id_type=MESH
                        )
                        greeted += 1

    def send(src, dst, send_sem, recv_sem, target):
        pltpu.make_async_remote_copy(
            src_ref=src, dst_ref=dst, send_sem=send_sem, recv_sem=recv_sem,
            device_id=target, device_id_type=MESH,
        ).start()

    phase_load.wait()

    def first_tables(i, carry):
        cos, sin = turn_tables(lpv[i], True)
        for k in range(2):
            cos1[k, i] = cos[k]
            sin1[k, i] = sin[k]
        return carry

    lax.fori_loop(0, 128, first_tables, 0)

    def rotate_first(c):
        left, half = c // 2, c % 2
        if half == 0:
            loads[left].wait()

        def step(i, carry):
            for vx in range(4):
                box = i * 4 + vx
                direct = None
                crossed = None
                for k in range(2):
                    value = cbuf[left, box, k, pl.ds(half * 8, 8), :]
                    d = value * cos1[k, box, pl.ds(left, 1), :]
                    e = value * sin1[k, box, pl.ds(left, 1), :]
                    direct = d if direct is None else direct + d
                    crossed = e if crossed is None else crossed + e
                sendx[c, vx, i] = direct + swap(crossed)
            return carry

        lax.fori_loop(0, 32, step, 0)

    def send_x(c):
        for dx in range(1, 4):
            there = (x + dx) % 4
            send(sendx.at[c, there], recvx.at[c, x], x_send.at[c], x_recv.at[c], (big_x, y * 4 + there))

    rotate_first(0)
    pl.semaphore_wait(barrier, greeted)
    send_x(0)

    me_in = big_x * 4 + y

    def send_phase(d, carry):
        there_x = ((z + d // 8) % 4) * 2 + (core + (d // 4) % 2) % 2
        there_y = (y + d % 4) % 4
        send(
            lpv.at[pl.ds((there_x * 4 + there_y) * 4, 4)], p1.at[me_in], ph_send.at[0], ph_recv.at[0],
            (there_x, there_y * 4 + x),
        )
        return carry

    lax.fori_loop(1, 32, send_phase, 0)
    for vx in range(4):
        p1[me_in, vx] = lpv[me_in * 4 + vx]

    for c in range(1, 4):
        rotate_first(c)
        if c == 1:
            wait_for(p1.at[pl.ds(0, 31)], ph_recv.at[0])
            for dx in range(1, 4):
                there = (x + dx) % 4
                send(p1.at[:, there], phs.at[:, x], ph_send.at[1], ph_recv.at[1], (big_x, y * 4 + there))
        send_x(c)

    def pass_on(c):
        wait_for(recvx.at[c, pl.ds(0, 3)], x_recv.at[c])

        def own(i, carry):
            recvx[c, x, i] = sendx[c, x, i]
            return carry

        lax.fori_loop(0, 32, own, 0)

        def add(i, carry):
            for y1 in range(2):
                send1[c, i, y1] = recvx[c, 2 * y1, i] + recvx[c, 2 * y1 + 1, i]
            return carry

        lax.fori_loop(0, 32, add, 0)

        def push(d, carry):
            there_x = ((z + d // 8) % 4) * 2 + (core + (d // 4) % 2) % 2
            there_y = (y + d % 4) % 4
            send(
                send1.at[c, there_x * 4 + there_y], recv1.at[c, me_in], in_send.at[c], in_recv.at[c],
                (there_x, there_y * 4 + x),
            )
            return carry

        lax.fori_loop(1, 32, push, 0)
        for y1 in range(2):
            recv1[c, me_in, y1] = send1[c, me_in, y1]

    def put_parts(row, value):
        high, low = split_parts(value)
        rows = pl.ds(pl.multiple_of(row, 16), 16)
        xs[rows, 0:WIDE] = high
        xs[rows, WIDE : 2 * WIDE] = low
        xs[rows, 2 * WIDE : 3 * WIDE] = high

    def multiply():
        def piece(i, carry):
            rows = pl.ds(pl.multiple_of(i * 256, 256), 256)
            res[rows, :] = jnp.dot(xs[rows, :], w_ref[...], preferred_element_type=F32)
            return carry

        lax.fori_loop(0, 2, piece, 0)

    def turned_sum(parts, row):
        direct = None
        crossed = None
        for block, column, k, place in parts:
            value = res[pl.ds(pl.multiple_of(block * 8, 8), 8), column * WIDE : (column + 1) * WIDE]
            d = value * cos_t[k, place, pl.ds(row, 1), :]
            e = value * sin_t[k, place, pl.ds(row, 1), :]
            direct = d if direct is None else direct + d
            crossed = e if crossed is None else crossed + e
        return direct + swap(crossed)

    def levels(c):
        left, half = c // 2, c % 2
        wait_for(recv1.at[c, pl.ds(0, 31)], in_recv.at[c])

        def first(i, carry):
            put_parts(i * 16, recv1[c, i].reshape(16, WIDE))
            return carry

        lax.fori_loop(0, 32, first, 0)
        multiply()
        if c == 0:
            phase_tables()

        def second(t, carry):
            x2, x1, y3, y2 = t // 8, (t // 4) % 2, (t // 2) % 2, t % 2
            for y0 in range(2):
                outs = []
                for k in range(2):
                    parts = []
                    for x0 in range(2):
                        for y1 in range(2):
                            block = x2 * 32 + x1 * 16 + x0 * 8 + y3 * 4 + y2 * 2 + y1
                            place = (x2 * 4 + x1 * 2 + x0) * 16 + y3 * 8 + y2 * 4 + y1 * 2 + y0
                            parts.append((block, k * 2 + y0, k, place))
                    outs.append(turned_sum(parts, 2 + left))
                put_parts((t * 2 + y0) * 16, jnp.concatenate(outs, axis=0))
            return carry

        lax.fori_loop(0, 16, second, 0)
        multiply()

        def third(t, carry):
            x2, y3, y0, k = t // 8, (t // 4) % 2, (t // 2) % 2, t % 2
            for x0 in range(2):
                outs = []
                for y1 in range(2):
                    parts = []
                    for x1 in range(2):
                        for y2 in range(2):
                            block = x2 * 32 + x1 * 16 + y3 * 8 + y2 * 4 + y0 * 2 + k
                            place = (x2 * 4 + x1 * 2 + x0) * 16 + y3 * 8 + y2 * 4 + y1 * 2 + y0
                            parts.append((block, x0 * 2 + y1, k, place))
                    outs.append(turned_sum(parts, 4 + left))
                put_parts((t * 2 + x0) * 16, jnp.concatenate(outs, axis=0))
            return carry

        lax.fori_loop(0, 16, third, 0)
        multiply()

        def fourth(t, carry):
            y0, k, x0, y1 = t // 8, (t // 4) % 2, (t // 2) % 2, t % 2
            for x1 in range(2):
                for y2 in range(2):
                    parts = []
                    for x2 in range(2):
                        for y3 in range(2):
                            block = x2 * 32 + y3 * 16 + y0 * 8 + k * 4 + x0 * 2 + y1
                            place = (x2 * 4 + x1 * 2 + x0) * 16 + y3 * 8 + y2 * 4 + y1 * 2 + y0
                            parts.append((block, x1 * 2 + y2, k, place))
                    if half == 0:
                        s4[c, x0 * 8 + y2 * 4 + y1 * 2 + y0, x1, k] = turned_sum(parts, 6 + left)
                    else:
                        s4[c, x1 * 8 + x0 * 4 + y1 * 2 + y0, y2, k] = turned_sum(parts, 6 + left)
            return carry

        lax.fori_loop(0, 16, fourth, 0)

    def phase_tables():
        wait_for(phs.at[:, pl.ds(0, 3)], ph_recv.at[1])

        def own(i, carry):
            phs[i, x] = p1[i, x]
            return carry

        lax.fori_loop(0, 32, own, 0)

        def table(i, carry):
            for sx in range(4):
                cos, sin = turn_tables(phs[i, sx], True)
                for k in range(2):
                    cos_t[k, i * 4 + sx] = cos[k]
                    sin_t[k, i * 4 + sx] = sin[k]
            return carry

        lax.fori_loop(0, 32, table, 0)

    def out_first(c):
        half = c % 2
        if half == 0:
            me = core * 16 + y * 4 + x

            def push(d, carry):
                there_c = (core + d // 16) % 2
                there_y = (y + (d // 4) % 4) % 4
                there_x = (x + d % 4) % 4
                send(
                    s4.at[c, there_c * 8 + (there_y % 2) * 4 + there_x], r1.at[c, me],
                    s1_send.at[c], s1_recv.at[c], (z * 2 + there_c, there_y * 4 + there_x),
                )
                return carry

            mine = core * 8 + (y % 2) * 4 + x
        else:
            me = (z * 2 + core) * 4 + x

            def push(d, carry):
                there_c = (core + d // 16) % 2
                there_z = (z + (d // 4) % 4) % 4
                there_x = (x + d % 4) % 4
                send(
                    s4.at[c, (there_z % 2) * 8 + there_c * 4 + there_x], r1.at[c, me],
                    s1_send.at[c], s1_recv.at[c], (there_z * 2 + there_c, y * 4 + there_x),
                )
                return carry

            mine = (z % 2) * 8 + core * 4 + x
        lax.fori_loop(1, 32, push, 0)
        for a in range(2):
            for b in range(2):
                r1[c, me, a, b] = s4[c, mine, a, b]

    def out_last(c):
        left, half = c // 2, c % 2
        wait_for(r1.at[c, pl.ds(0, 31)], s1_recv.at[c])
        got, pos = (gz, z) if half == 0 else (gy, y)
        for d in (2, 1, 3):
            there = (pos + d) % 4
            target = (there * 2 + core, big_y) if half == 0 else (big_x, there * 4 + x)
            send(r1.at[c, :, there % 2], got.at[left, pos], s2_send.at[c], s2_recv.at[c], target)
        own = pltpu.make_async_copy(r1.at[c, :, pos % 2], got.at[left, pos], own_sem.at[c])
        own.start()

    def finish(c):
        left, half = c // 2, c % 2
        got, pos = (gz, z) if half == 0 else (gy, y)
        wait_for(got.at[left, pl.ds(0, 3)], s2_recv.at[c])
        pltpu.make_async_copy(r1.at[c, :, pos % 2], got.at[left, pos], own_sem.at[c]).wait()

    pass_on(0)
    levels(0)
    out_first(0)
    pass_on(1)
    levels(1)
    out_first(1)
    pass_on(2)
    out_last(0)
    levels(2)
    out_first(2)
    pass_on(3)
    out_last(1)
    levels(3)
    out_first(3)
    out_last(2)
    out_last(3)
    for c in range(4):
        finish(c)
        wait_for(sendx.at[c, pl.ds(0, 3)], x_send.at[c])
        wait_for(send1.at[c, pl.ds(0, 31)], in_send.at[c])
        wait_for(r1.at[c, pl.ds(0, 31)], s1_send.at[c])
        wait_for(gz.at[0, pl.ds(0, 3)], s2_send.at[c])
    wait_for(p1.at[pl.ds(0, 31)], ph_send.at[0])
    wait_for(phs.at[:, pl.ds(0, 3)], ph_send.at[1])


def exchange(coeffs, phases, spread):
    half = jax.ShapeDtypeStruct((2, 4, 32, 2, 8, WIDE), F32)
    dma = pltpu.SemaphoreType.DMA
    return pl.pallas_call(
        exchange_kernel,
        out_shape=(half, half),
        in_specs=[
            pl.BlockSpec(memory_space=pl.ANY),
            pl.BlockSpec(memory_space=pl.ANY),
            pl.BlockSpec(memory_space=pltpu.VMEM),
        ],
        out_specs=(pl.BlockSpec(memory_space=pl.ANY), pl.BlockSpec(memory_space=pl.ANY)),
        scratch_shapes=[
            pltpu.VMEM((2, 128, 2, 16, WIDE), F32),
            pltpu.VMEM((128, 8, WIDE), F32),
            pltpu.VMEM((2, 128, 8, WIDE), F32),
            pltpu.VMEM((2, 128, 8, WIDE), F32),
            pltpu.VMEM((4, 4, 32, 8, WIDE), F32),
            pltpu.VMEM((4, 4, 32, 8, WIDE), F32),
            pltpu.VMEM((4, 32, 2, 8, WIDE), F32),
            pltpu.VMEM((4, 32, 2, 8, WIDE), F32),
            pltpu.VMEM((32, 4, 8, WIDE), F32),
            pltpu.VMEM((32, 4, 8, WIDE), F32),
            pltpu.VMEM((2, 128, 8, WIDE), F32),
            pltpu.VMEM((2, 128, 8, WIDE), F32),
            pltpu.VMEM((512, 3 * WIDE), BF16),
            pltpu.VMEM((512, 4 * WIDE), F32),
            pltpu.VMEM((4, 16, 2, 2, 8, WIDE), F32),
            pltpu.VMEM((4, 32, 2, 2, 8, WIDE), F32),
            dma((3,)),
            dma((4,)),
            dma((4,)),
            dma((4,)),
            dma((4,)),
            dma((4,)),
            dma((4,)),
            dma((4,)),
            dma((4,)),
            dma((4,)),
            dma((2,)),
            dma((2,)),
        ],
        compiler_params=pltpu.CompilerParams(
            collective_id=0, has_side_effects=True, vmem_limit_bytes=48 * 2**20
        ),
        name="exchange",
    )(coeffs, phases, spread)


def field_kernel(gz, gy, angles, w_ref, out, cos_f, sin_f):
    q = lax.axis_index("qx") // 4
    s = lax.axis_index("qy") // 8
    cos, sin = turn_tables(angles[0], False)
    for k in range(2):
        cos_f[k] = cos[k]
        sin_f[k] = sin[k]
    matrix = w_ref.at[q * 2 + s]

    def step(sy, carry):
        pieces = []
        for sx in range(4):
            for left in range(2):
                for k in range(2):
                    pieces.append(gz[left, 0, sy * 4 + sx, k])
                    pieces.append(gy[left, sy, sx, k])
        high, low = split_parts(jnp.concatenate(pieces, axis=0))
        both = jnp.dot(
            jnp.concatenate([high, low, high], axis=1), matrix[...], preferred_element_type=F32
        )
        at = 0
        for sx in range(4):
            for left in range(2):
                row = pl.ds((sy * 4 + sx) * 2 + left, 1)
                for k in range(2):
                    direct = both[at : at + 16, :WIDE]
                    crossed = both[at : at + 16, WIDE:]
                    out[0, sy * 4 + sx, left, k] = direct * cos_f[k, row, :] + crossed * sin_f[k, row, :]
                    at += 16
        return carry

    lax.fori_loop(0, 4, step, 0)


def evaluate_field(gz, gy, angles, last):
    return pl.pallas_call(
        field_kernel,
        grid=(8,),
        out_shape=jax.ShapeDtypeStruct((8, 16, 2, 2, 16, WIDE), F32),
        in_specs=[
            pl.BlockSpec((2, 1, 16, 2, 8, WIDE), lambda h: (0, h // 2, h % 2, 0, 0, 0)),
            pl.BlockSpec((2, 4, 4, 2, 8, WIDE), lambda h: (0, 0, h, 0, 0, 0)),
            pl.BlockSpec((1, 32, WIDE), lambda h: (h, 0, 0)),
            pl.BlockSpec((4, 3 * WIDE, 2 * WIDE), lambda h: (0, 0, 0)),
        ],
        out_specs=pl.BlockSpec((1, 16, 2, 2, 16, WIDE), lambda h: (h, 0, 0, 0, 0, 0)),
        scratch_shapes=[pltpu.VMEM((2, 32, WIDE), F32), pltpu.VMEM((2, 32, WIDE), F32)],
        compiler_params=pltpu.CompilerParams(vmem_limit_bytes=32 * 2**20),
        name="field",
    )(gz, gy, angles, last)


def per_device(coeffs, level_phase, field_phase):
    spread, last = weights()
    gz, gy = exchange(
        coeffs.reshape(128, 2, 2, 16, WIDE), level_phase.reshape(128, 8, WIDE), spread
    )
    field = evaluate_field(gz, gy, field_phase.reshape(8, 32, WIDE), last)
    return field.reshape(coeffs.shape)


def solution(mesh):
    return jax.shard_map(
        per_device,
        mesh=mesh,
        in_specs=(
            P("qx", "qy", None, None, None, None, None, None),
            P("qx", "qy", None, None, None, None, None),
            P("qx", "qy", None, None, None, None),
        ),
        out_specs=P("qx", "qy", None, None, None, None, None, None),
        check_vma=False,
    )
```

```python
import functools

import jax
import jax.numpy as jnp
import numpy as np
from jax import lax
from jax.experimental import pallas as pl
from jax.experimental.pallas import tpu as pltpu
from jax.sharding import PartitionSpec as P

CHEB = 8
PTS = CHEB * CHEB
WIDE = 2 * PTS
MESH = pl.DeviceIdType.MESH
F32 = jnp.float32
BF16 = jnp.bfloat16
DIGITS = [(a, b, c) for a in range(2) for b in range(2) for c in range(2)]


def point_tables(count):
    points = 0.5 - 0.5 * np.cos((2 * np.arange(count) + 1) * np.pi / (2 * count))

    def lagrange(places):
        values = np.ones((len(places), count))
        for k in range(count):
            for m in range(count):
                if m != k:
                    values[:, k] = values[:, k] * (places - points[m]) / (points[k] - points[m])
        return values

    halves = [lagrange((q + points) / 2.0) for q in range(2)]
    uniform = lagrange((np.arange(count) + 0.5) / count)
    identity = np.eye(2)
    children = [
        [np.kron(identity, np.kron(halves[q], halves[s])).T for s in range(2)] for q in range(2)
    ]
    evaluate = np.kron(identity, np.kron(uniform, uniform)).T
    return children, evaluate


def three_parts(matrix):
    high = matrix.astype(np.float32).astype(BF16)
    low = (matrix - high.astype(np.float64)).astype(np.float32).astype(BF16)
    return np.concatenate([high, high, low], axis=0)


def weights():
    children, evaluate = point_tables(CHEB)
    spread = three_parts(np.concatenate([children[q][s] for q in range(2) for s in range(2)], axis=1))
    last = []
    for q in range(2):
        for s in range(2):
            both = children[q][s] @ evaluate
            swapped = np.concatenate([both[:, PTS:], both[:, :PTS]], axis=1)
            last.append(three_parts(np.concatenate([both, swapped], axis=1)))
    return jnp.asarray(spread), jnp.asarray(np.stack(last))


def split_parts(value):
    high = value.astype(BF16)
    low = (value - high.astype(F32)).astype(BF16)
    return high, low


def sine_cosine(angle):
    u = angle * 0.5
    w = u * u
    s = -2.5052108e-08
    for c in (2.7557319e-06, -1.9841270e-04, 8.3333333e-03, -1.6666667e-01, 1.0):
        s = s * w + c
    s = s * u
    c_ = 2.0876757e-09
    for c in (-2.7557319e-07, 2.4801587e-05, -1.3888889e-03, 4.1666667e-02, -0.5, 1.0):
        c_ = c_ * w + c
    return 2.0 * s * c_, 1.0 - 2.0 * s * s


def swap(value):
    return pltpu.roll(value, PTS, value.ndim - 1)


def turn_tables(angle, before):
    sine, cosine = sine_cosine(angle)
    lane = lax.broadcasted_iota(jnp.int32, angle.shape, angle.ndim - 1)
    low = lane < PTS
    cos_swap, sin_swap = swap(cosine), swap(sine)
    cos = (jnp.where(low, cosine, cos_swap), jnp.where(low, cos_swap, cosine))
    if before:
        sin = (jnp.where(low, sine, -sin_swap), jnp.where(low, sin_swap, -sine))
    else:
        sin = (jnp.where(low, -sine, sin_swap), jnp.where(low, -sin_swap, sine))
    return cos, sin


def wait_for(ref, sem):
    pltpu.make_async_copy(ref, ref, sem).wait()


def exchange_kernel(
    coeffs, phases, w_ref, gz, gy,
    cbuf, lpv, cos1, sin1, sendx, recvx, send1, recv1, p1, phs, cos_t, sin_t, xs, res, s4, r1,
    load_sem, x_send, x_recv, in_send, in_recv, s1_send, s1_recv, s2_send, s2_recv, own_sem,
    ph_send, ph_recv,
):
    big_x = lax.axis_index("qx")
    big_y = lax.axis_index("qy")
    z, core = big_x // 2, big_x % 2
    y, x = big_y // 4, big_y % 4

    phase_load = pltpu.make_async_copy(phases, lpv, load_sem.at[2])
    phase_load.start()
    loads = []
    for left in range(2):
        load = pltpu.make_async_copy(coeffs.at[:, left], cbuf.at[left], load_sem.at[left])
        load.start()
        loads.append(load)

    zs = [(z + d) % 4 for d in range(4)]
    cs = [core, 1 - core]
    ys = [(y + d) % 4 for d in range(4)]
    xs_ = [(x + d) % 4 for d in range(4)]
    y_odd = [(y + d) % 2 for d in range(4)]
    z_odd = [(z + d) % 2 for d in range(4)]
    dev_x = [[zs[dz] * 2 + cs[dc] for dc in range(2)] for dz in range(4)]
    dev_y = [[ys[dy] * 4 + xs_[dx] for dx in range(4)] for dy in range(4)]

    barrier = pltpu.get_barrier_semaphore()
    greeted = 0
    for dz in range(4):
        for dc in range(2):
            for dy in range(4):
                for dx in range(4):
                    if (dz, dc, dy, dx) != (0, 0, 0, 0) and 0 in (dz, dy, dx):
                        pl.semaphore_signal(
                            barrier, inc=1, device_id=(dev_x[dz][dc], dev_y[dy][dx]), device_id_type=MESH
                        )
                        greeted += 1

    def send(src, dst, send_sem, recv_sem, target):
        pltpu.make_async_remote_copy(
            src_ref=src, dst_ref=dst, send_sem=send_sem, recv_sem=recv_sem,
            device_id=target, device_id_type=MESH,
        ).start()

    phase_load.wait()

    def first_tables(i, carry):
        some = pl.ds(i * 8, 8)
        cos, sin = turn_tables(lpv[some], True)
        for k in range(2):
            cos1[k, some] = cos[k]
            sin1[k, some] = sin[k]
        return carry

    lax.fori_loop(0, 16, first_tables, 0)

    def rotate_first(c):
        left, half = c // 2, c % 2
        if half == 0:
            loads[left].wait()

        def step(j, carry):
            for n in range(16):
                i = j * 4 + n // 4
                vx = n % 4
                box = j * 16 + n
                direct = None
                crossed = None
                for k in range(2):
                    value = cbuf[left, box, k, pl.ds(half * 8, 8), :]
                    d = value * cos1[k, box, pl.ds(left, 1), :]
                    e = value * sin1[k, box, pl.ds(left, 1), :]
                    direct = d if direct is None else direct + d
                    crossed = e if crossed is None else crossed + e
                sendx[c, vx, i] = direct + swap(crossed)
            return carry

        lax.fori_loop(0, 8, step, 0)

    def send_x(c):
        for dx in range(1, 4):
            there = xs_[dx]
            send(sendx.at[c, there], recvx.at[c, x], x_send.at[c], x_recv.at[c], (big_x, y * 4 + there))

    rotate_first(0)
    pl.semaphore_wait(barrier, greeted)
    send_x(0)

    me_in = big_x * 4 + y

    for d in range(1, 32):
        there_x = dev_x[d // 8][(d // 4) % 2]
        send(
            lpv.at[pl.ds(there_x * 16 + ys[d % 4] * 4, 4)], p1.at[me_in], ph_send.at[0], ph_recv.at[0],
            (there_x, dev_y[d % 4][0]),
        )
    for vx in range(4):
        p1[me_in, vx] = lpv[me_in * 4 + vx]

    for c in range(1, 4):
        rotate_first(c)
        if c == 1:
            wait_for(p1.at[pl.ds(0, 31)], ph_recv.at[0])
            for dx in range(1, 4):
                there = xs_[dx]
                send(p1.at[:, there], phs.at[:, x], ph_send.at[1], ph_recv.at[1], (big_x, y * 4 + there))
        send_x(c)

    def pass_on(c):
        wait_for(recvx.at[c, pl.ds(0, 3)], x_recv.at[c])

        recvx[c, x] = sendx[c, x]

        def add(j, carry):
            some = pl.ds(j * 8, 8)
            for y1 in range(2):
                send1[c, some, y1] = recvx[c, 2 * y1, some] + recvx[c, 2 * y1 + 1, some]
            return carry

        lax.fori_loop(0, 4, add, 0)

        for d in range(1, 32):
            there_x = dev_x[d // 8][(d // 4) % 2]
            send(
                send1.at[c, there_x * 4 + ys[d % 4]], recv1.at[c, me_in], in_send.at[c], in_recv.at[c],
                (there_x, dev_y[d % 4][0]),
            )
        for y1 in range(2):
            recv1[c, me_in, y1] = send1[c, me_in, y1]

    def put_parts(row, value):
        high, low = split_parts(value)
        rows = pl.ds(pl.multiple_of(row, 16), 16)
        xs[rows, 0:WIDE] = high
        xs[rows, WIDE : 2 * WIDE] = low
        xs[rows, 2 * WIDE : 3 * WIDE] = high

    def multiply():
        def piece(i, carry):
            rows = pl.ds(pl.multiple_of(i * 256, 256), 256)
            res[rows, :] = jnp.dot(xs[rows, :], w_ref[...], preferred_element_type=F32)
            return carry

        lax.fori_loop(0, 2, piece, 0)

    def turned_sum(parts, row):
        direct = None
        crossed = None
        for block, column, k, place in parts:
            value = res[pl.ds(pl.multiple_of(block * 8, 8), 8), column * WIDE : (column + 1) * WIDE]
            d = value * cos_t[k, place, pl.ds(row, 1), :]
            e = value * sin_t[k, place, pl.ds(row, 1), :]
            direct = d if direct is None else direct + d
            crossed = e if crossed is None else crossed + e
        return direct + swap(crossed)

    def levels(c):
        left, half = c // 2, c % 2
        wait_for(recv1.at[c, pl.ds(0, 31)], in_recv.at[c])

        def first(j, carry):
            for n in range(8):
                i = j * 8 + n
                put_parts(i * 16, recv1[c, i].reshape(16, WIDE))
            return carry

        lax.fori_loop(0, 4, first, 0)
        multiply()
        if c == 0:
            phase_tables()

        def second(a, carry):
            for y3, y2, y0 in DIGITS:
                outs = []
                for k in range(2):
                    parts = []
                    for x0 in range(2):
                        for y1 in range(2):
                            block = a * 16 + (x0 * 8 + y3 * 4 + y2 * 2 + y1)
                            place = a * 32 + (x0 * 16 + y3 * 8 + y2 * 4 + y1 * 2 + y0)
                            parts.append((block, k * 2 + y0, k, place))
                    outs.append(turned_sum(parts, 2 + left))
                put_parts(a * 128 + (y3 * 4 + y2 * 2 + y0) * 16, jnp.concatenate(outs, axis=0))
            return carry

        lax.fori_loop(0, 4, second, 0)
        multiply()

        def third(x2, carry):
            for y3, y0, k in DIGITS:
                for x0 in range(2):
                    outs = []
                    for y1 in range(2):
                        parts = []
                        for x1 in range(2):
                            for y2 in range(2):
                                block = x2 * 32 + (x1 * 16 + y3 * 8 + y2 * 4 + y0 * 2 + k)
                                place = x2 * 64 + (x1 * 32 + x0 * 16 + y3 * 8 + y2 * 4 + y1 * 2 + y0)
                                parts.append((block, x0 * 2 + y1, k, place))
                        outs.append(turned_sum(parts, 4 + left))
                    put_parts(
                        x2 * 256 + (y3 * 8 + y0 * 4 + k * 2 + x0) * 16, jnp.concatenate(outs, axis=0)
                    )
            return carry

        lax.fori_loop(0, 2, third, 0)
        multiply()

        def fourth(y0, carry):
            for k, x0, y1 in DIGITS:
                for x1 in range(2):
                    for y2 in range(2):
                        parts = []
                        for x2 in range(2):
                            for y3 in range(2):
                                block = y0 * 8 + (x2 * 32 + y3 * 16 + k * 4 + x0 * 2 + y1)
                                place = y0 + (x2 * 64 + x1 * 32 + x0 * 16 + y3 * 8 + y2 * 4 + y1 * 2)
                                parts.append((block, x1 * 2 + y2, k, place))
                        if half == 0:
                            s4[c, y0 + (x0 * 8 + y2 * 4 + y1 * 2), x1, k] = turned_sum(parts, 6 + left)
                        else:
                            s4[c, y0 + (x1 * 8 + x0 * 4 + y1 * 2), y2, k] = turned_sum(parts, 6 + left)
            return carry

        lax.fori_loop(0, 2, fourth, 0)

    def phase_tables():
        wait_for(phs.at[:, pl.ds(0, 3)], ph_recv.at[1])

        phs[:, x] = p1[:, x]

        def table(i, carry):
            some = pl.ds(i * 8, 8)
            angle = phs[pl.ds(i * 2, 2)].reshape(8, 8, WIDE)
            cos, sin = turn_tables(angle, True)
            for k in range(2):
                cos_t[k, some] = cos[k]
                sin_t[k, some] = sin[k]
            return carry

        lax.fori_loop(0, 16, table, 0)

    def out_first(c):
        half = c % 2
        if half == 0:
            me = core * 16 + y * 4 + x
            mine = core * 8 + (y % 2) * 4 + x
        else:
            me = (z * 2 + core) * 4 + x
            mine = (z % 2) * 8 + core * 4 + x
        for d in range(1, 32):
            dc, dx, dt = d // 16, d % 4, (d // 4) % 4
            if half == 0:
                there = cs[dc] * 8 + y_odd[dt] * 4 + xs_[dx]
                target = (dev_x[0][dc], dev_y[dt][dx])
            else:
                there = z_odd[dt] * 8 + cs[dc] * 4 + xs_[dx]
                target = (dev_x[dt][dc], dev_y[0][dx])
            send(s4.at[c, there], r1.at[c, me], s1_send.at[c], s1_recv.at[c], target)
        for a in range(2):
            for b in range(2):
                r1[c, me, a, b] = s4[c, mine, a, b]

    def out_last(c):
        left, half = c // 2, c % 2
        wait_for(r1.at[c, pl.ds(0, 31)], s1_recv.at[c])
        got, pos = (gz, z) if half == 0 else (gy, y)
        for d in (2, 1, 3):
            odd = z_odd[d] if half == 0 else y_odd[d]
            target = (dev_x[d][0], big_y) if half == 0 else (big_x, dev_y[d][0])
            send(r1.at[c, :, odd], got.at[left, pos], s2_send.at[c], s2_recv.at[c], target)
        own = pltpu.make_async_copy(r1.at[c, :, pos % 2], got.at[left, pos], own_sem.at[c])
        own.start()

    def finish(c):
        left, half = c // 2, c % 2
        got, pos = (gz, z) if half == 0 else (gy, y)
        wait_for(got.at[left, pl.ds(0, 3)], s2_recv.at[c])
        pltpu.make_async_copy(r1.at[c, :, pos % 2], got.at[left, pos], own_sem.at[c]).wait()

    pass_on(0)
    levels(0)
    out_first(0)
    pass_on(1)
    levels(1)
    out_first(1)
    pass_on(2)
    out_last(0)
    levels(2)
    out_first(2)
    pass_on(3)
    out_last(1)
    levels(3)
    out_first(3)
    out_last(2)
    out_last(3)
    for c in range(4):
        finish(c)
        wait_for(sendx.at[c, pl.ds(0, 3)], x_send.at[c])
        wait_for(send1.at[c, pl.ds(0, 31)], in_send.at[c])
        wait_for(r1.at[c, pl.ds(0, 31)], s1_send.at[c])
        wait_for(gz.at[0, pl.ds(0, 3)], s2_send.at[c])
    wait_for(p1.at[pl.ds(0, 31)], ph_send.at[0])
    wait_for(phs.at[:, pl.ds(0, 3)], ph_send.at[1])


def exchange(coeffs, phases, spread):
    half = jax.ShapeDtypeStruct((2, 4, 32, 2, 8, WIDE), F32)
    dma = pltpu.SemaphoreType.DMA
    return pl.pallas_call(
        exchange_kernel,
        out_shape=(half, half),
        in_specs=[
            pl.BlockSpec(memory_space=pl.ANY),
            pl.BlockSpec(memory_space=pl.ANY),
            pl.BlockSpec(memory_space=pltpu.VMEM),
        ],
        out_specs=(pl.BlockSpec(memory_space=pl.ANY), pl.BlockSpec(memory_space=pl.ANY)),
        scratch_shapes=[
            pltpu.VMEM((2, 128, 2, 16, WIDE), F32),
            pltpu.VMEM((128, 8, WIDE), F32),
            pltpu.VMEM((2, 128, 8, WIDE), F32),
            pltpu.VMEM((2, 128, 8, WIDE), F32),
            pltpu.VMEM((4, 4, 32, 8, WIDE), F32),
            pltpu.VMEM((4, 4, 32, 8, WIDE), F32),
            pltpu.VMEM((4, 32, 2, 8, WIDE), F32),
            pltpu.VMEM((4, 32, 2, 8, WIDE), F32),
            pltpu.VMEM((32, 4, 8, WIDE), F32),
            pltpu.VMEM((32, 4, 8, WIDE), F32),
            pltpu.VMEM((2, 128, 8, WIDE), F32),
            pltpu.VMEM((2, 128, 8, WIDE), F32),
            pltpu.VMEM((512, 3 * WIDE), BF16),
            pltpu.VMEM((512, 4 * WIDE), F32),
            pltpu.VMEM((4, 16, 2, 2, 8, WIDE), F32),
            pltpu.VMEM((4, 32, 2, 2, 8, WIDE), F32),
            dma((3,)),
            dma((4,)),
            dma((4,)),
            dma((4,)),
            dma((4,)),
            dma((4,)),
            dma((4,)),
            dma((4,)),
            dma((4,)),
            dma((4,)),
            dma((2,)),
            dma((2,)),
        ],
        compiler_params=pltpu.CompilerParams(
            collective_id=0, has_side_effects=True, vmem_limit_bytes=48 * 2**20
        ),
        name="exchange",
    )(coeffs, phases, spread)


def field_kernel(gz, gy, angles, w_ref, out, cos_f, sin_f):
    q = lax.axis_index("qx") // 4
    s = lax.axis_index("qy") // 8
    cos, sin = turn_tables(angles[0], False)
    for k in range(2):
        cos_f[k] = cos[k]
        sin_f[k] = sin[k]
    matrix = w_ref.at[q * 2 + s]

    def step(sy, carry):
        pieces = []
        for sx in range(4):
            for left in range(2):
                for k in range(2):
                    pieces.append(gz[left, 0, sy * 4 + sx, k])
                    pieces.append(gy[left, sy, sx, k])
        high, low = split_parts(jnp.concatenate(pieces, axis=0))
        both = jnp.dot(
            jnp.concatenate([high, low, high], axis=1), matrix[...], preferred_element_type=F32
        )
        at = 0
        for sx in range(4):
            for left in range(2):
                row = pl.ds((sy * 4 + sx) * 2 + left, 1)
                for k in range(2):
                    direct = both[at : at + 16, :WIDE]
                    crossed = both[at : at + 16, WIDE:]
                    out[0, sy * 4 + sx, left, k] = direct * cos_f[k, row, :] + crossed * sin_f[k, row, :]
                    at += 16
        return carry

    lax.fori_loop(0, 4, step, 0)


def evaluate_field(gz, gy, angles, last):
    return pl.pallas_call(
        field_kernel,
        grid=(8,),
        out_shape=jax.ShapeDtypeStruct((8, 16, 2, 2, 16, WIDE), F32),
        in_specs=[
            pl.BlockSpec((2, 1, 16, 2, 8, WIDE), lambda h: (0, h // 2, h % 2, 0, 0, 0)),
            pl.BlockSpec((2, 4, 4, 2, 8, WIDE), lambda h: (0, 0, h, 0, 0, 0)),
            pl.BlockSpec((1, 32, WIDE), lambda h: (h, 0, 0)),
            pl.BlockSpec((4, 3 * WIDE, 2 * WIDE), lambda h: (0, 0, 0)),
        ],
        out_specs=pl.BlockSpec((1, 16, 2, 2, 16, WIDE), lambda h: (h, 0, 0, 0, 0, 0)),
        scratch_shapes=[pltpu.VMEM((2, 32, WIDE), F32), pltpu.VMEM((2, 32, WIDE), F32)],
        compiler_params=pltpu.CompilerParams(vmem_limit_bytes=32 * 2**20),
        name="field",
    )(gz, gy, angles, last)


def per_device(coeffs, level_phase, field_phase):
    spread, last = weights()
    gz, gy = exchange(
        coeffs.reshape(128, 2, 2, 16, WIDE), level_phase.reshape(128, 8, WIDE), spread
    )
    field = evaluate_field(gz, gy, field_phase.reshape(8, 32, WIDE), last)
    return field.reshape(coeffs.shape)


def solution(mesh):
    return jax.shard_map(
        per_device,
        mesh=mesh,
        in_specs=(
            P("qx", "qy", None, None, None, None, None, None),
            P("qx", "qy", None, None, None, None, None),
            P("qx", "qy", None, None, None, None),
        ),
        out_specs=P("qx", "qy", None, None, None, None, None, None),
        check_vma=False,
    )
```

```python
import functools

import jax
import jax.numpy as jnp
import numpy as np
from jax import lax
from jax.experimental import pallas as pl
from jax.experimental.pallas import tpu as pltpu
from jax.sharding import PartitionSpec as P

CHEB = 8
PTS = CHEB * CHEB
WIDE = 2 * PTS
MESH = pl.DeviceIdType.MESH
F32 = jnp.float32
BF16 = jnp.bfloat16
DIGITS = [(a, b, c) for a in range(2) for b in range(2) for c in range(2)]


def point_tables(count):
    points = 0.5 - 0.5 * np.cos((2 * np.arange(count) + 1) * np.pi / (2 * count))

    def lagrange(places):
        values = np.ones((len(places), count))
        for k in range(count):
            for m in range(count):
                if m != k:
                    values[:, k] = values[:, k] * (places - points[m]) / (points[k] - points[m])
        return values

    halves = [lagrange((q + points) / 2.0) for q in range(2)]
    uniform = lagrange((np.arange(count) + 0.5) / count)
    identity = np.eye(2)
    children = [
        [np.kron(identity, np.kron(halves[q], halves[s])).T for s in range(2)] for q in range(2)
    ]
    evaluate = np.kron(identity, np.kron(uniform, uniform)).T
    return children, evaluate


def three_parts(matrix):
    high = matrix.astype(np.float32).astype(BF16)
    low = (matrix - high.astype(np.float64)).astype(np.float32).astype(BF16)
    return np.concatenate([high, high, low], axis=0)


def weights():
    children, evaluate = point_tables(CHEB)
    spread = three_parts(np.concatenate([children[q][s] for q in range(2) for s in range(2)], axis=1))
    last = []
    for q in range(2):
        for s in range(2):
            both = children[q][s] @ evaluate
            swapped = np.concatenate([both[:, PTS:], both[:, :PTS]], axis=1)
            last.append(three_parts(np.concatenate([both, swapped], axis=1)))
    return jnp.asarray(spread), jnp.asarray(np.stack(last))


def split_parts(value):
    high = value.astype(BF16)
    low = (value - high.astype(F32)).astype(BF16)
    return high, low


def sine_cosine(angle):
    u = angle * 0.5
    w = u * u
    s = -2.5052108e-08
    for c in (2.7557319e-06, -1.9841270e-04, 8.3333333e-03, -1.6666667e-01, 1.0):
        s = s * w + c
    s = s * u
    c_ = 2.0876757e-09
    for c in (-2.7557319e-07, 2.4801587e-05, -1.3888889e-03, 4.1666667e-02, -0.5, 1.0):
        c_ = c_ * w + c
    return 2.0 * s * c_, 1.0 - 2.0 * s * s


def swap(value):
    return pltpu.roll(value, PTS, value.ndim - 1)


def turn_tables(angle, before):
    sine, cosine = sine_cosine(angle)
    lane = lax.broadcasted_iota(jnp.int32, angle.shape, angle.ndim - 1)
    low = lane < PTS
    cos_swap, sin_swap = swap(cosine), swap(sine)
    cos = (jnp.where(low, cosine, cos_swap), jnp.where(low, cos_swap, cosine))
    if before:
        sin = (jnp.where(low, sine, -sin_swap), jnp.where(low, sin_swap, -sine))
    else:
        sin = (jnp.where(low, -sine, sin_swap), jnp.where(low, -sin_swap, sine))
    return cos, sin


def wait_for(ref, sem):
    pltpu.make_async_copy(ref, ref, sem).wait()


def butterfly_kernel(
    coeffs, phases, field_phases, w_all, w_last, out,
    cbuf, lpv, fpv, w_ref, wf_ref, cos1, sin1, cos_f, sin_f,
    send_a, recv_xa, send_ya, recv_ya, send_yb, recv_yb, recv_xb,
    p1, phs, cos_t, sin_t, xs, res, s4, r1, gz, gy,
    load_sem, x_send, x_recv, in_send, in_recv, s1_send, s1_recv, s2_send, s2_recv, ph_send, ph_recv,
):
    big_x = lax.axis_index("qx")
    big_y = lax.axis_index("qy")
    z, core = big_x // 2, big_x % 2
    y, x = big_y // 4, big_y % 4
    pick = (z // 2) * 2 + y // 2

    loads = [
        pltpu.make_async_copy(src, dst, load_sem.at[n])
        for n, (src, dst) in enumerate(
            [
                (phases, lpv),
                (coeffs.at[:, 0], cbuf.at[0]),
                (coeffs.at[:, 1], cbuf.at[1]),
                (w_all, w_ref),
                (field_phases, fpv),
                (w_last.at[pick], wf_ref),
            ]
        )
    ]
    for load in loads:
        load.start()

    zs = [(z + d) % 4 for d in range(4)]
    cs = [core, 1 - core]
    ys = [(y + d) % 4 for d in range(4)]
    xs_ = [(x + d) % 4 for d in range(4)]
    y_odd = [(y + d) % 2 for d in range(4)]
    z_odd = [(z + d) % 2 for d in range(4)]
    dev_x = [[zs[dz] * 2 + cs[dc] for dc in range(2)] for dz in range(4)]
    dev_y = [[ys[dy] * 4 + xs_[dx] for dx in range(4)] for dy in range(4)]

    barrier = pltpu.get_barrier_semaphore()
    greeted = 0
    for dz in range(4):
        for dc in range(2):
            for dy in range(4):
                for dx in range(4):
                    if (dz, dc, dy, dx) != (0, 0, 0, 0) and 0 in (dz, dy, dx):
                        pl.semaphore_signal(
                            barrier, inc=1, device_id=(dev_x[dz][dc], dev_y[dy][dx]), device_id_type=MESH
                        )
                        greeted += 1

    def send(src, dst, send_sem, recv_sem, target):
        pltpu.make_async_remote_copy(
            src_ref=src, dst_ref=dst, send_sem=send_sem, recv_sem=recv_sem,
            device_id=target, device_id_type=MESH,
        ).start()

    me_in = big_x * 4 + y
    me_z = core * 16 + y * 4 + x
    me_y = big_x * 4 + x

    loads[0].wait()

    def first_tables(i, carry):
        some = pl.ds(i * 8, 8)
        cos, sin = turn_tables(lpv[some], True)
        for k in range(2):
            cos1[k, some] = cos[k]
            sin1[k, some] = sin[k]
        return carry

    lax.fori_loop(0, 16, first_tables, 0)

    def rotate_first(c):
        left, half = c // 2, c % 2
        if half == 0:
            loads[1 + left].wait()

        def step(j, carry):
            for n in range(16):
                i = j * 4 + n // 4
                vx = n % 4
                box = j * 16 + n
                direct = None
                crossed = None
                for k in range(2):
                    value = cbuf[left, box, k, pl.ds(half * 8, 8), :]
                    d = value * cos1[k, box, pl.ds(left, 1), :]
                    e = value * sin1[k, box, pl.ds(left, 1), :]
                    direct = d if direct is None else direct + d
                    crossed = e if crossed is None else crossed + e
                if left == 0:
                    send_a[half, vx, i] = direct + swap(crossed)
                else:
                    send_yb[half, i, vx] = direct + swap(crossed)
            return carry

        lax.fori_loop(0, 8, step, 0)

    def send_x(src, dst, send_sem, recv_sem):
        for dx in range(1, 4):
            send(src(xs_[dx]), dst, send_sem, recv_sem, (big_x, dev_y[0][dx]))

    def send_in(src, dst, send_sem, recv_sem):
        for d in range(1, 32):
            there_x = dev_x[d // 8][(d // 4) % 2]
            send(src(there_x * 4 + ys[d % 4]), dst, send_sem, recv_sem, (there_x, dev_y[d % 4][0]))

    def enter(c):
        h = c % 2
        if c < 2:
            send_x(lambda t: send_a.at[h, t], recv_xa.at[h, x], x_send.at[c], x_recv.at[c])
        else:
            send_in(lambda t: send_yb.at[h, t], recv_yb.at[h, me_in], in_send.at[c], in_recv.at[c])

    def pass_on(c):
        h = c % 2
        if c < 2:
            wait_for(recv_xa.at[h, pl.ds(0, 3)], x_recv.at[c])
            recv_xa[h, x] = send_a[h, x]

            def add(j, carry):
                some = pl.ds(j * 8, 8)
                for y1 in range(2):
                    send_ya[h, some, y1] = recv_xa[h, 2 * y1, some] + recv_xa[h, 2 * y1 + 1, some]
                return carry

            lax.fori_loop(0, 4, add, 0)
            send_in(lambda t: send_ya.at[h, t], recv_ya.at[h, me_in], in_send.at[c], in_recv.at[c])
            recv_ya[h, me_in] = send_ya[h, me_in]
        else:
            wait_for(recv_yb.at[h, pl.ds(0, 31)], in_recv.at[c])
            recv_yb[h, me_in] = send_yb[h, me_in]
            send_x(lambda t: recv_yb.at[h, :, t], recv_xb.at[h, x], x_send.at[c], x_recv.at[c])
            recv_xb[h, x] = recv_yb[h, :, x]

    def send_phases():
        send_in(lambda t: lpv.at[pl.ds(t * 4, 4)], p1.at[me_in], ph_send.at[0], ph_recv.at[0])
        p1[me_in] = lpv[pl.ds(me_in * 4, 4)]

    def pass_phases():
        wait_for(p1.at[pl.ds(0, 31)], ph_recv.at[0])
        send_x(lambda t: p1.at[:, t], phs.at[:, x], ph_send.at[1], ph_recv.at[1])
        phs[:, x] = p1[:, x]

    def phase_tables():
        wait_for(phs.at[:, pl.ds(0, 3)], ph_recv.at[1])

        def table(i, carry):
            some = pl.ds(i * 8, 8)
            angle = phs[pl.ds(i * 2, 2)].reshape(8, 8, WIDE)
            cos, sin = turn_tables(angle, True)
            for k in range(2):
                cos_t[k, some] = cos[k]
                sin_t[k, some] = sin[k]
            return carry

        lax.fori_loop(0, 16, table, 0)

    def field_tables():
        loads[4].wait()

        def table(i, carry):
            cos, sin = turn_tables(fpv[i], False)
            for k in range(2):
                cos_f[k, i] = cos[k]
                sin_f[k, i] = sin[k]
            return carry

        lax.fori_loop(0, 8, table, 0)

    def put_parts(row, value):
        high, low = split_parts(value)
        rows = pl.ds(pl.multiple_of(row, 16), 16)
        xs[rows, 0:WIDE] = high
        xs[rows, WIDE : 2 * WIDE] = low
        xs[rows, 2 * WIDE : 3 * WIDE] = high

    def multiply():
        def piece(i, carry):
            rows = pl.ds(pl.multiple_of(i * 256, 256), 256)
            res[rows, :] = jnp.dot(xs[rows, :], w_ref[...], preferred_element_type=F32)
            return carry

        lax.fori_loop(0, 2, piece, 0)

    def turned_sum(parts, row):
        direct = None
        crossed = None
        for block, column, k, place in parts:
            value = res[pl.ds(pl.multiple_of(block * 8, 8), 8), column * WIDE : (column + 1) * WIDE]
            d = value * cos_t[k, place, pl.ds(row, 1), :]
            e = value * sin_t[k, place, pl.ds(row, 1), :]
            direct = d if direct is None else direct + d
            crossed = e if crossed is None else crossed + e
        return direct + swap(crossed)

    def level_one(c):
        h = c % 2
        if c < 2:
            wait_for(recv_ya.at[h, pl.ds(0, 31)], in_recv.at[c])
        else:
            wait_for(recv_xb.at[h, pl.ds(0, 3)], x_recv.at[c])

        def first(j, carry):
            for n in range(8):
                i = j * 8 + n
                if c < 2:
                    value = recv_ya[h, i].reshape(16, WIDE)
                else:
                    value = jnp.concatenate(
                        [recv_xb[h, 2 * y1, i] + recv_xb[h, 2 * y1 + 1, i] for y1 in range(2)], axis=0
                    )
                put_parts(i * 16, value)
            return carry

        lax.fori_loop(0, 4, first, 0)
        multiply()

    def other_levels(c):
        left = c // 2

        def second(a, carry):
            for y3, y2, y0 in DIGITS:
                outs = []
                for k in range(2):
                    parts = []
                    for x0 in range(2):
                        for y1 in range(2):
                            block = a * 16 + (x0 * 8 + y3 * 4 + y2 * 2 + y1)
                            place = a * 32 + (x0 * 16 + y3 * 8 + y2 * 4 + y1 * 2 + y0)
                            parts.append((block, k * 2 + y0, k, place))
                    outs.append(turned_sum(parts, 2 + left))
                put_parts(a * 128 + (y3 * 4 + y2 * 2 + y0) * 16, jnp.concatenate(outs, axis=0))
            return carry

        lax.fori_loop(0, 4, second, 0)
        multiply()

        def third(x2, carry):
            for y3, y0, k in DIGITS:
                for x0 in range(2):
                    outs = []
                    for y1 in range(2):
                        parts = []
                        for x1 in range(2):
                            for y2 in range(2):
                                block = x2 * 32 + (x1 * 16 + y3 * 8 + y2 * 4 + y0 * 2 + k)
                                place = x2 * 64 + (x1 * 32 + x0 * 16 + y3 * 8 + y2 * 4 + y1 * 2 + y0)
                                parts.append((block, x0 * 2 + y1, k, place))
                        outs.append(turned_sum(parts, 4 + left))
                    put_parts(
                        x2 * 256 + (y3 * 8 + y0 * 4 + k * 2 + x0) * 16, jnp.concatenate(outs, axis=0)
                    )
            return carry

        lax.fori_loop(0, 2, third, 0)
        multiply()

        def fourth(y0, carry):
            for k, x0, y1 in DIGITS:
                for x1 in range(2):
                    for y2 in range(2):
                        parts = []
                        for x2 in range(2):
                            for y3 in range(2):
                                block = y0 * 8 + (x2 * 32 + y3 * 16 + k * 4 + x0 * 2 + y1)
                                place = y0 + (x2 * 64 + x1 * 32 + x0 * 16 + y3 * 8 + y2 * 4 + y1 * 2)
                                parts.append((block, x1 * 2 + y2, k, place))
                        if k == 0:
                            s4[c, 0, y0 + (x0 * 8 + y2 * 4 + y1 * 2), x1] = turned_sum(parts, 6 + left)
                        else:
                            s4[c, 1, y0 + (x1 * 8 + x0 * 4 + y1 * 2), y2] = turned_sum(parts, 6 + left)
            return carry

        lax.fori_loop(0, 2, fourth, 0)

        for d in range(1, 32):
            dc, dt, dx = d // 16, (d // 4) % 4, d % 4
            send(
                s4.at[c, 0, cs[dc] * 8 + y_odd[dt] * 4 + xs_[dx]], r1.at[c, 0, me_z],
                s1_send.at[c, 0], s1_recv.at[c, 0], (dev_x[0][dc], dev_y[dt][dx]),
            )
            send(
                s4.at[c, 1, z_odd[dt] * 8 + cs[dc] * 4 + xs_[dx]], r1.at[c, 1, me_y],
                s1_send.at[c, 1], s1_recv.at[c, 1], (dev_x[dt][dc], dev_y[0][dx]),
            )
        r1[c, 0, me_z] = s4[c, 0, core * 8 + y_odd[0] * 4 + x]
        r1[c, 1, me_y] = s4[c, 1, z_odd[0] * 8 + core * 4 + x]

    def out_last(c, k):
        wait_for(r1.at[c, k, pl.ds(0, 31)], s1_recv.at[c, k])
        for d in (2, 1, 3):
            if k == 0:
                send(
                    r1.at[c, 0, :, z_odd[d]], gz.at[c, z], s2_send.at[c, 0], s2_recv.at[c, 0],
                    (dev_x[d][0], big_y),
                )
            else:
                send(
                    r1.at[c, 1, :, y_odd[d]], gy.at[c, y], s2_send.at[c, 1], s2_recv.at[c, 1],
                    (big_x, dev_y[d][0]),
                )
        if k == 0:
            gz[c, z] = r1[c, 0, :, z_odd[0]]
        else:
            gy[c, y] = r1[c, 1, :, y_odd[0]]

    def finish(c, k):
        left, half = c // 2, c % 2
        got = gz if k == 0 else gy
        wait_for(got.at[c, pl.ds(0, 3)], s2_recv.at[c, k])

        def piece(p, carry):
            for a in range(2):
                for n in range(16):
                    put_parts((a * 16 + n) * 16, got[c, p * 2 + a, pl.ds(2 * n, 2)].reshape(16, WIDE))
            res[:, 0 : 2 * WIDE] = jnp.dot(xs[...], wf_ref[...], preferred_element_type=F32)
            for a in range(2):
                for n in range(32):
                    if k == 0:
                        box_h, box_v = p * 4 + (a * 2 + n // 16), n % 16
                    else:
                        box_h, box_v = n // 4, p * 8 + (a * 4 + n % 4)
                    rows = slice((a * 32 + n) * 8, (a * 32 + n + 1) * 8)
                    at = pl.ds(box_v * 2 + left, 1)
                    out[box_h * 16 + box_v, left, k, pl.ds(half * 8, 8), :] = (
                        res[rows, 0:WIDE] * cos_f[k, box_h, at, :]
                        + res[rows, WIDE : 2 * WIDE] * sin_f[k, box_h, at, :]
                    )
            return carry

        lax.fori_loop(0, 2, piece, 0)

    rotate_first(0)
    pl.semaphore_wait(barrier, greeted)
    enter(0)
    send_phases()
    rotate_first(1)
    enter(1)
    rotate_first(2)
    enter(2)
    pass_on(0)
    pass_phases()
    rotate_first(3)
    enter(3)
    pass_on(1)
    pass_on(2)
    loads[3].wait()
    field_tables()
    level_one(0)
    phase_tables()
    other_levels(0)
    level_one(1)
    pass_on(3)
    other_levels(1)
    out_last(0, 0)
    out_last(0, 1)
    level_one(2)
    other_levels(2)
    level_one(3)
    out_last(1, 0)
    out_last(1, 1)
    other_levels(3)
    out_last(2, 0)
    out_last(2, 1)
    loads[5].wait()
    finish(0, 0)
    finish(0, 1)
    out_last(3, 0)
    out_last(3, 1)
    for c in range(1, 4):
        finish(c, 0)
        finish(c, 1)
    for c in range(4):
        h = c % 2
        wait_for(recv_xa.at[h, pl.ds(0, 3)], x_send.at[c])
        wait_for((recv_ya if c < 2 else recv_yb).at[h, pl.ds(0, 31)], in_send.at[c])
        for k in range(2):
            wait_for(r1.at[c, k, pl.ds(0, 31)], s1_send.at[c, k])
            wait_for(gz.at[c, pl.ds(0, 3)], s2_send.at[c, k])
    wait_for(p1.at[pl.ds(0, 31)], ph_send.at[0])
    wait_for(phs.at[:, pl.ds(0, 3)], ph_send.at[1])


def butterfly(coeffs, phases, field_phases, spread, last):
    dma = pltpu.SemaphoreType.DMA
    tile = (8, WIDE)

    def vmem(*shape):
        return pltpu.VMEM(shape + tile, F32)

    return pl.pallas_call(
        butterfly_kernel,
        out_shape=jax.ShapeDtypeStruct((128, 2, 2, 16, WIDE), F32),
        in_specs=[pl.BlockSpec(memory_space=pltpu.HBM)] * 5,
        out_specs=pl.BlockSpec(memory_space=pltpu.VMEM),
        scratch_shapes=[
            pltpu.VMEM((2, 128, 2, 16, WIDE), F32),
            vmem(128),
            pltpu.VMEM((8, 32, WIDE), F32),
            pltpu.VMEM((3 * WIDE, 4 * WIDE), BF16),
            pltpu.VMEM((3 * WIDE, 2 * WIDE), BF16),
            vmem(2, 128),
            vmem(2, 128),
            pltpu.VMEM((2, 8, 32, WIDE), F32),
            pltpu.VMEM((2, 8, 32, WIDE), F32),
            vmem(2, 4, 32),
            vmem(2, 4, 32),
            vmem(2, 32, 2),
            vmem(2, 32, 2),
            vmem(2, 32, 4),
            vmem(2, 32, 4),
            vmem(2, 4, 32),
            vmem(32, 4),
            vmem(32, 4),
            vmem(2, 128),
            vmem(2, 128),
            pltpu.VMEM((512, 3 * WIDE), BF16),
            pltpu.VMEM((512, 4 * WIDE), F32),
            vmem(4, 2, 16, 2),
            vmem(4, 2, 32, 2),
            vmem(4, 4, 32),
            vmem(4, 4, 32),
            dma((6,)),
            dma((4,)),
            dma((4,)),
            dma((4,)),
            dma((4,)),
            dma((4, 2)),
            dma((4, 2)),
            dma((4, 2)),
            dma((4, 2)),
            dma((2,)),
            dma((2,)),
        ],
        compiler_params=pltpu.CompilerParams(
            collective_id=0, has_side_effects=True, vmem_limit_bytes=48 * 2**20
        ),
        name="butterfly",
    )(coeffs, phases, field_phases, spread, last)


def per_device(coeffs, level_phase, field_phase):
    spread, last = weights()
    field = butterfly(
        coeffs.reshape(128, 2, 2, 16, WIDE), level_phase.reshape(128, 8, WIDE),
        field_phase.reshape(8, 32, WIDE), spread, last,
    )
    return field.reshape(coeffs.shape)


def solution(mesh):
    return jax.shard_map(
        per_device,
        mesh=mesh,
        in_specs=(
            P("qx", "qy", None, None, None, None, None, None),
            P("qx", "qy", None, None, None, None, None),
            P("qx", "qy", None, None, None, None),
        ),
        out_specs=P("qx", "qy", None, None, None, None, None, None),
        check_vma=False,
    )
```

```python
import functools

import jax
import jax.numpy as jnp
import numpy as np
from jax import lax
from jax.experimental import pallas as pl
from jax.experimental.pallas import tpu as pltpu
from jax.sharding import PartitionSpec as P

CHEB = 8
PTS = CHEB * CHEB
WIDE = 2 * PTS
MESH = pl.DeviceIdType.MESH
F32 = jnp.float32
BF16 = jnp.bfloat16
DIGITS = [(a, b, c) for a in range(2) for b in range(2) for c in range(2)]


def point_tables(count):
    points = 0.5 - 0.5 * np.cos((2 * np.arange(count) + 1) * np.pi / (2 * count))

    def lagrange(places):
        values = np.ones((len(places), count))
        for k in range(count):
            for m in range(count):
                if m != k:
                    values[:, k] = values[:, k] * (places - points[m]) / (points[k] - points[m])
        return values

    halves = [lagrange((q + points) / 2.0) for q in range(2)]
    uniform = lagrange((np.arange(count) + 0.5) / count)
    identity = np.eye(2)
    children = [
        [np.kron(identity, np.kron(halves[q], halves[s])).T for s in range(2)] for q in range(2)
    ]
    evaluate = np.kron(identity, np.kron(uniform, uniform)).T
    return children, evaluate


def three_parts(matrix):
    high = matrix.astype(np.float32).astype(BF16)
    low = (matrix - high.astype(np.float64)).astype(np.float32).astype(BF16)
    return np.concatenate([high, high, low], axis=0)


def weights():
    children, evaluate = point_tables(CHEB)
    spread = three_parts(np.concatenate([children[q][s] for q in range(2) for s in range(2)], axis=1))
    last = []
    for q in range(2):
        for s in range(2):
            both = children[q][s] @ evaluate
            swapped = np.concatenate([both[:, PTS:], both[:, :PTS]], axis=1)
            last.append(three_parts(np.concatenate([both, swapped], axis=1)))
    return jnp.asarray(spread), jnp.asarray(np.stack(last))


def split_parts(value):
    high = value.astype(BF16)
    low = (value - high.astype(F32)).astype(BF16)
    return high, low


def sine_cosine(angle):
    u = angle * 0.5
    w = u * u
    s = -2.5052108e-08
    for c in (2.7557319e-06, -1.9841270e-04, 8.3333333e-03, -1.6666667e-01, 1.0):
        s = s * w + c
    s = s * u
    c_ = 2.0876757e-09
    for c in (-2.7557319e-07, 2.4801587e-05, -1.3888889e-03, 4.1666667e-02, -0.5, 1.0):
        c_ = c_ * w + c
    return 2.0 * s * c_, 1.0 - 2.0 * s * s


def swap(value):
    return pltpu.roll(value, PTS, value.ndim - 1)


def turn_tables(angle, before):
    sine, cosine = sine_cosine(angle)
    lane = lax.broadcasted_iota(jnp.int32, angle.shape, angle.ndim - 1)
    low = lane < PTS
    cos_swap, sin_swap = swap(cosine), swap(sine)
    cos = (jnp.where(low, cosine, cos_swap), jnp.where(low, cos_swap, cosine))
    if before:
        sin = (jnp.where(low, sine, -sin_swap), jnp.where(low, sin_swap, -sine))
    else:
        sin = (jnp.where(low, -sine, sin_swap), jnp.where(low, -sin_swap, sine))
    return cos, sin


def wait_for(ref, sem):
    pltpu.make_async_copy(ref, ref, sem).wait()


def butterfly_kernel(
    coeffs, phases, field_phases, w_all, w_last, out,
    cbuf, lpv, fpv, w_ref, wf_ref, cos1, sin1, cos_f, sin_f,
    send_a, recv_xa, send_ya, recv_ya, send_yb, recv_yb, recv_xb,
    p1, phs, cos_t, sin_t, xs, res, s4, r1, gz, gy, done,
    load_sem, out_sem, x_send, x_recv, in_send, in_recv, s1_send, s1_recv, s2_send, s2_recv, ph_send, ph_recv,
):
    big_x = lax.axis_index("qx")
    big_y = lax.axis_index("qy")
    z, core = big_x // 2, big_x % 2
    y, x = big_y // 4, big_y % 4
    pick = (z // 2) * 2 + y // 2

    loads = [
        pltpu.make_async_copy(src, dst, load_sem.at[n])
        for n, (src, dst) in enumerate(
            [
                (phases, lpv),
                (coeffs.at[:, 0], cbuf.at[0]),
                (coeffs.at[:, 1], cbuf.at[1]),
                (w_all, w_ref),
                (field_phases, fpv),
                (w_last.at[pick], wf_ref),
            ]
        )
    ]
    for load in loads:
        load.start()

    zs = [(z + d) % 4 for d in range(4)]
    cs = [core, 1 - core]
    ys = [(y + d) % 4 for d in range(4)]
    xs_ = [(x + d) % 4 for d in range(4)]
    y_odd = [(y + d) % 2 for d in range(4)]
    z_odd = [(z + d) % 2 for d in range(4)]
    dev_x = [[zs[dz] * 2 + cs[dc] for dc in range(2)] for dz in range(4)]
    dev_y = [[ys[dy] * 4 + xs_[dx] for dx in range(4)] for dy in range(4)]

    barrier = pltpu.get_barrier_semaphore()
    greeted = 0
    for dz in range(4):
        for dc in range(2):
            for dy in range(4):
                for dx in range(4):
                    if (dz, dc, dy, dx) != (0, 0, 0, 0) and 0 in (dz, dy, dx):
                        pl.semaphore_signal(
                            barrier, inc=1, device_id=(dev_x[dz][dc], dev_y[dy][dx]), device_id_type=MESH
                        )
                        greeted += 1

    def send(src, dst, send_sem, recv_sem, target):
        pltpu.make_async_remote_copy(
            src_ref=src, dst_ref=dst, send_sem=send_sem, recv_sem=recv_sem,
            device_id=target, device_id_type=MESH,
        ).start()

    me_in = big_x * 4 + y
    me_z = core * 16 + y * 4 + x
    me_y = big_x * 4 + x

    loads[0].wait()

    def first_tables(i, carry):
        some = pl.ds(i * 8, 8)
        cos, sin = turn_tables(lpv[some], True)
        for k in range(2):
            cos1[k, some] = cos[k]
            sin1[k, some] = sin[k]
        return carry

    lax.fori_loop(0, 16, first_tables, 0)

    def rotate_first(c):
        left, half = c // 2, c % 2
        if half == 0:
            loads[1 + left].wait()

        def step(j, carry):
            for n in range(16):
                i = j * 4 + n // 4
                vx = n % 4
                box = j * 16 + n
                direct = None
                crossed = None
                for k in range(2):
                    value = cbuf[left, box, k, pl.ds(half * 8, 8), :]
                    d = value * cos1[k, box, pl.ds(left, 1), :]
                    e = value * sin1[k, box, pl.ds(left, 1), :]
                    direct = d if direct is None else direct + d
                    crossed = e if crossed is None else crossed + e
                if left == 0:
                    send_a[half, vx, i] = direct + swap(crossed)
                else:
                    send_yb[half, i, vx] = direct + swap(crossed)
            return carry

        lax.fori_loop(0, 8, step, 0)

    def send_x(src, dst, send_sem, recv_sem):
        for dx in range(1, 4):
            send(src(xs_[dx]), dst, send_sem, recv_sem, (big_x, dev_y[0][dx]))

    def send_in(src, dst, send_sem, recv_sem):
        for d in range(1, 32):
            there_x = dev_x[d // 8][(d // 4) % 2]
            send(src(there_x * 4 + ys[d % 4]), dst, send_sem, recv_sem, (there_x, dev_y[d % 4][0]))

    def enter(c):
        h = c % 2
        if c < 2:
            send_x(lambda t: send_a.at[h, t], recv_xa.at[h, x], x_send.at[c], x_recv.at[c])
        else:
            send_in(lambda t: send_yb.at[h, t], recv_yb.at[h, me_in], in_send.at[c], in_recv.at[c])

    def pass_on(c):
        h = c % 2
        if c < 2:
            wait_for(recv_xa.at[h, pl.ds(0, 3)], x_recv.at[c])
            recv_xa[h, x] = send_a[h, x]

            def add(j, carry):
                some = pl.ds(j * 8, 8)
                for y1 in range(2):
                    send_ya[h, some, y1] = recv_xa[h, 2 * y1, some] + recv_xa[h, 2 * y1 + 1, some]
                return carry

            lax.fori_loop(0, 4, add, 0)
            send_in(lambda t: send_ya.at[h, t], recv_ya.at[h, me_in], in_send.at[c], in_recv.at[c])
            recv_ya[h, me_in] = send_ya[h, me_in]
        else:
            wait_for(recv_yb.at[h, pl.ds(0, 31)], in_recv.at[c])
            recv_yb[h, me_in] = send_yb[h, me_in]
            send_x(lambda t: recv_yb.at[h, :, t], recv_xb.at[h, x], x_send.at[c], x_recv.at[c])
            recv_xb[h, x] = recv_yb[h, :, x]

    def send_phases():
        send_in(lambda t: lpv.at[pl.ds(t * 4, 4)], p1.at[me_in], ph_send.at[0], ph_recv.at[0])
        p1[me_in] = lpv[pl.ds(me_in * 4, 4)]

    def pass_phases():
        wait_for(p1.at[pl.ds(0, 31)], ph_recv.at[0])
        send_x(lambda t: p1.at[:, t], phs.at[:, x], ph_send.at[1], ph_recv.at[1])
        phs[:, x] = p1[:, x]

    def phase_tables():
        wait_for(phs.at[:, pl.ds(0, 3)], ph_recv.at[1])

        def table(i, carry):
            some = pl.ds(i * 8, 8)
            angle = phs[pl.ds(i * 2, 2)].reshape(8, 8, WIDE)
            cos, sin = turn_tables(angle, True)
            for k in range(2):
                cos_t[k, some] = cos[k]
                sin_t[k, some] = sin[k]
            return carry

        lax.fori_loop(0, 16, table, 0)

    def field_tables():
        loads[4].wait()

        def table(i, carry):
            cos, sin = turn_tables(fpv[i], False)
            for k in range(2):
                cos_f[k, i] = cos[k]
                sin_f[k, i] = sin[k]
            return carry

        lax.fori_loop(0, 8, table, 0)

    def put_parts(row, value):
        high, low = split_parts(value)
        rows = pl.ds(pl.multiple_of(row, 16), 16)
        xs[rows, 0:WIDE] = high
        xs[rows, WIDE : 2 * WIDE] = low
        xs[rows, 2 * WIDE : 3 * WIDE] = high

    def multiply():
        def piece(i, carry):
            rows = pl.ds(pl.multiple_of(i * 256, 256), 256)
            res[rows, :] = jnp.dot(xs[rows, :], w_ref[...], preferred_element_type=F32)
            return carry

        lax.fori_loop(0, 2, piece, 0)

    def turned_sum(parts, row):
        direct = None
        crossed = None
        for block, column, k, place in parts:
            value = res[pl.ds(pl.multiple_of(block * 8, 8), 8), column * WIDE : (column + 1) * WIDE]
            d = value * cos_t[k, place, pl.ds(row, 1), :]
            e = value * sin_t[k, place, pl.ds(row, 1), :]
            direct = d if direct is None else direct + d
            crossed = e if crossed is None else crossed + e
        return direct + swap(crossed)

    def level_one(c):
        h = c % 2
        if c < 2:
            wait_for(recv_ya.at[h, pl.ds(0, 31)], in_recv.at[c])
        else:
            wait_for(recv_xb.at[h, pl.ds(0, 3)], x_recv.at[c])

        def first(j, carry):
            for n in range(8):
                i = j * 8 + n
                if c < 2:
                    value = recv_ya[h, i].reshape(16, WIDE)
                else:
                    value = jnp.concatenate(
                        [recv_xb[h, 2 * y1, i] + recv_xb[h, 2 * y1 + 1, i] for y1 in range(2)], axis=0
                    )
                put_parts(i * 16, value)
            return carry

        lax.fori_loop(0, 4, first, 0)
        multiply()

    def other_levels(c):
        left = c // 2

        def second(a, carry):
            for y3, y2, y0 in DIGITS:
                outs = []
                for k in range(2):
                    parts = []
                    for x0 in range(2):
                        for y1 in range(2):
                            block = a * 16 + (x0 * 8 + y3 * 4 + y2 * 2 + y1)
                            place = a * 32 + (x0 * 16 + y3 * 8 + y2 * 4 + y1 * 2 + y0)
                            parts.append((block, k * 2 + y0, k, place))
                    outs.append(turned_sum(parts, 2 + left))
                put_parts(a * 128 + (y3 * 4 + y2 * 2 + y0) * 16, jnp.concatenate(outs, axis=0))
            return carry

        lax.fori_loop(0, 4, second, 0)
        multiply()

        def third(x2, carry):
            for y3, y0, k in DIGITS:
                for x0 in range(2):
                    outs = []
                    for y1 in range(2):
                        parts = []
                        for x1 in range(2):
                            for y2 in range(2):
                                block = x2 * 32 + (x1 * 16 + y3 * 8 + y2 * 4 + y0 * 2 + k)
                                place = x2 * 64 + (x1 * 32 + x0 * 16 + y3 * 8 + y2 * 4 + y1 * 2 + y0)
                                parts.append((block, x0 * 2 + y1, k, place))
                        outs.append(turned_sum(parts, 4 + left))
                    put_parts(
                        x2 * 256 + (y3 * 8 + y0 * 4 + k * 2 + x0) * 16, jnp.concatenate(outs, axis=0)
                    )
            return carry

        lax.fori_loop(0, 2, third, 0)
        multiply()

        def fourth(y0, carry):
            for k, x0, y1 in DIGITS:
                for x1 in range(2):
                    for y2 in range(2):
                        parts = []
                        for x2 in range(2):
                            for y3 in range(2):
                                block = y0 * 8 + (x2 * 32 + y3 * 16 + k * 4 + x0 * 2 + y1)
                                place = y0 + (x2 * 64 + x1 * 32 + x0 * 16 + y3 * 8 + y2 * 4 + y1 * 2)
                                parts.append((block, x1 * 2 + y2, k, place))
                        if k == 0:
                            s4[c, 0, y0 + (x0 * 8 + y2 * 4 + y1 * 2), x1] = turned_sum(parts, 6 + left)
                        else:
                            s4[c, 1, y0 + (x1 * 8 + x0 * 4 + y1 * 2), y2] = turned_sum(parts, 6 + left)
            return carry

        lax.fori_loop(0, 2, fourth, 0)

        for d in range(1, 32):
            dc, dt, dx = d // 16, (d // 4) % 4, d % 4
            send(
                s4.at[c, 0, cs[dc] * 8 + y_odd[dt] * 4 + xs_[dx]], r1.at[c, 0, me_z],
                s1_send.at[c, 0], s1_recv.at[c, 0], (dev_x[0][dc], dev_y[dt][dx]),
            )
            send(
                s4.at[c, 1, z_odd[dt] * 8 + cs[dc] * 4 + xs_[dx]], r1.at[c, 1, me_y],
                s1_send.at[c, 1], s1_recv.at[c, 1], (dev_x[dt][dc], dev_y[0][dx]),
            )
        r1[c, 0, me_z] = s4[c, 0, core * 8 + y_odd[0] * 4 + x]
        r1[c, 1, me_y] = s4[c, 1, z_odd[0] * 8 + core * 4 + x]

    def out_last(c, k):
        wait_for(r1.at[c, k, pl.ds(0, 31)], s1_recv.at[c, k])
        for d in (2, 1, 3):
            if k == 0:
                send(
                    r1.at[c, 0, :, z_odd[d]], gz.at[c, z], s2_send.at[c, 0], s2_recv.at[c, 0],
                    (dev_x[d][0], big_y),
                )
            else:
                send(
                    r1.at[c, 1, :, y_odd[d]], gy.at[c, y], s2_send.at[c, 1], s2_recv.at[c, 1],
                    (big_x, dev_y[d][0]),
                )
        if k == 0:
            gz[c, z] = r1[c, 0, :, z_odd[0]]
        else:
            gy[c, y] = r1[c, 1, :, y_odd[0]]

    def finish(c, k):
        left, half = c // 2, c % 2
        got = gz if k == 0 else gy
        wait_for(got.at[c, pl.ds(0, 3)], s2_recv.at[c, k])

        def piece(p, carry):
            for a in range(2):
                for n in range(16):
                    put_parts((a * 16 + n) * 16, got[c, p * 2 + a, pl.ds(2 * n, 2)].reshape(16, WIDE))
            res[:, 0 : 2 * WIDE] = jnp.dot(xs[...], wf_ref[...], preferred_element_type=F32)
            for a in range(2):
                for n in range(32):
                    if k == 0:
                        box_h, box_v = p * 4 + (a * 2 + n // 16), n % 16
                    else:
                        box_h, box_v = n // 4, p * 8 + (a * 4 + n % 4)
                    rows = slice((a * 32 + n) * 8, (a * 32 + n + 1) * 8)
                    at = pl.ds(box_v * 2 + left, 1)
                    done[c, k, box_h * 16 + box_v] = (
                        res[rows, 0:WIDE] * cos_f[k, box_h, at, :]
                        + res[rows, WIDE : 2 * WIDE] * sin_f[k, box_h, at, :]
                    )
            return carry

        lax.fori_loop(0, 2, piece, 0)
        store = pltpu.make_async_copy(
            done.at[c, k], out.at[:, left, k, pl.ds(half * 8, 8)], out_sem.at[c, k]
        )
        store.start()
        stores.append(store)

    stores = []
    rotate_first(0)
    pl.semaphore_wait(barrier, greeted)
    enter(0)
    send_phases()
    rotate_first(1)
    enter(1)
    rotate_first(2)
    enter(2)
    pass_on(0)
    pass_phases()
    rotate_first(3)
    enter(3)
    pass_on(1)
    pass_on(2)
    loads[3].wait()
    field_tables()
    level_one(0)
    phase_tables()
    other_levels(0)
    level_one(1)
    pass_on(3)
    other_levels(1)
    out_last(0, 0)
    out_last(0, 1)
    level_one(2)
    other_levels(2)
    level_one(3)
    out_last(1, 0)
    out_last(1, 1)
    other_levels(3)
    out_last(2, 0)
    out_last(2, 1)
    loads[5].wait()
    finish(0, 0)
    finish(0, 1)
    out_last(3, 0)
    out_last(3, 1)
    for c in range(1, 4):
        finish(c, 0)
        finish(c, 1)
    for c in range(4):
        h = c % 2
        wait_for(recv_xa.at[h, pl.ds(0, 3)], x_send.at[c])
        wait_for((recv_ya if c < 2 else recv_yb).at[h, pl.ds(0, 31)], in_send.at[c])
        for k in range(2):
            wait_for(r1.at[c, k, pl.ds(0, 31)], s1_send.at[c, k])
            wait_for(gz.at[c, pl.ds(0, 3)], s2_send.at[c, k])
    for store in stores:
        store.wait()
    wait_for(p1.at[pl.ds(0, 31)], ph_send.at[0])
    wait_for(phs.at[:, pl.ds(0, 3)], ph_send.at[1])


def butterfly(coeffs, phases, field_phases, spread, last):
    dma = pltpu.SemaphoreType.DMA
    tile = (8, WIDE)

    def vmem(*shape):
        return pltpu.VMEM(shape + tile, F32)

    return pl.pallas_call(
        butterfly_kernel,
        out_shape=jax.ShapeDtypeStruct((128, 2, 2, 16, WIDE), F32),
        in_specs=[pl.BlockSpec(memory_space=pltpu.HBM)] * 5,
        out_specs=pl.BlockSpec(memory_space=pltpu.HBM),
        scratch_shapes=[
            pltpu.VMEM((2, 128, 2, 16, WIDE), F32),
            vmem(128),
            pltpu.VMEM((8, 32, WIDE), F32),
            pltpu.VMEM((3 * WIDE, 4 * WIDE), BF16),
            pltpu.VMEM((3 * WIDE, 2 * WIDE), BF16),
            vmem(2, 128),
            vmem(2, 128),
            pltpu.VMEM((2, 8, 32, WIDE), F32),
            pltpu.VMEM((2, 8, 32, WIDE), F32),
            vmem(2, 4, 32),
            vmem(2, 4, 32),
            vmem(2, 32, 2),
            vmem(2, 32, 2),
            vmem(2, 32, 4),
            vmem(2, 32, 4),
            vmem(2, 4, 32),
            vmem(32, 4),
            vmem(32, 4),
            vmem(2, 128),
            vmem(2, 128),
            pltpu.VMEM((512, 3 * WIDE), BF16),
            pltpu.VMEM((512, 4 * WIDE), F32),
            vmem(4, 2, 16, 2),
            vmem(4, 2, 32, 2),
            vmem(4, 4, 32),
            vmem(4, 4, 32),
            vmem(4, 2, 128),
            dma((6,)),
            dma((4, 2)),
            dma((4,)),
            dma((4,)),
            dma((4,)),
            dma((4,)),
            dma((4, 2)),
            dma((4, 2)),
            dma((4, 2)),
            dma((4, 2)),
            dma((2,)),
            dma((2,)),
        ],
        compiler_params=pltpu.CompilerParams(
            collective_id=0, has_side_effects=True, vmem_limit_bytes=60 * 2**20
        ),
        name="butterfly",
    )(coeffs, phases, field_phases, spread, last)


def hand_on_kernel(done, out, held, in_sem, out_sem):
    parts = in_sem.shape[0]
    rows = done.shape[0] // parts
    into, onto = [], []
    for n in range(parts):
        some = pl.ds(n * rows, rows)
        into.append(pltpu.make_async_copy(done.at[some], held.at[some], in_sem.at[n]))
        onto.append(pltpu.make_async_copy(held.at[some], out.at[some], out_sem.at[n]))
        into[n].start()
    for n in range(parts):
        into[n].wait()
        onto[n].start()
    for n in range(parts):
        onto[n].wait()


def hand_on(done, parts=4):
    return pl.pallas_call(
        hand_on_kernel,
        out_shape=jax.ShapeDtypeStruct(done.shape, F32),
        in_specs=[pl.BlockSpec(memory_space=pltpu.HBM)],
        out_specs=pl.BlockSpec(memory_space=pltpu.HBM),
        scratch_shapes=[
            pltpu.VMEM(done.shape, F32),
            pltpu.SemaphoreType.DMA((parts,)),
            pltpu.SemaphoreType.DMA((parts,)),
        ],
        compiler_params=pltpu.CompilerParams(vmem_limit_bytes=60 * 2**20),
        name="hand_on",
    )(done)


def per_device(coeffs, level_phase, field_phase):
    spread, last = weights()
    done = butterfly(
        coeffs.reshape(128, 2, 2, 16, WIDE), level_phase.reshape(128, 8, WIDE),
        field_phase.reshape(8, 32, WIDE), spread, last,
    )
    return hand_on(done).reshape(coeffs.shape)


def solution(mesh):
    return jax.shard_map(
        per_device,
        mesh=mesh,
        in_specs=(
            P("qx", "qy", None, None, None, None, None, None),
            P("qx", "qy", None, None, None, None, None),
            P("qx", "qy", None, None, None, None),
        ),
        out_specs=P("qx", "qy", None, None, None, None, None, None),
        check_vma=False,
    )
```

```python
import functools

import jax
import jax.numpy as jnp
import numpy as np
from jax import lax
from jax.experimental import pallas as pl
from jax.experimental.pallas import tpu as pltpu
from jax.sharding import PartitionSpec as P

CHEB = 8
PTS = CHEB * CHEB
WIDE = 2 * PTS
MESH = pl.DeviceIdType.MESH
F32 = jnp.float32
BF16 = jnp.bfloat16
DIGITS = [(a, b, c) for a in range(2) for b in range(2) for c in range(2)]


def point_tables(count):
    points = 0.5 - 0.5 * np.cos((2 * np.arange(count) + 1) * np.pi / (2 * count))

    def lagrange(places):
        values = np.ones((len(places), count))
        for k in range(count):
            for m in range(count):
                if m != k:
                    values[:, k] = values[:, k] * (places - points[m]) / (points[k] - points[m])
        return values

    halves = [lagrange((q + points) / 2.0) for q in range(2)]
    uniform = lagrange((np.arange(count) + 0.5) / count)
    identity = np.eye(2)
    children = [
        [np.kron(identity, np.kron(halves[q], halves[s])).T for s in range(2)] for q in range(2)
    ]
    evaluate = np.kron(identity, np.kron(uniform, uniform)).T
    return children, evaluate


def three_parts(matrix):
    high = matrix.astype(np.float32).astype(BF16)
    low = (matrix - high.astype(np.float64)).astype(np.float32).astype(BF16)
    return np.concatenate([high, high, low], axis=0)


def weights():
    children, evaluate = point_tables(CHEB)
    spread = three_parts(np.concatenate([children[q][s] for q in range(2) for s in range(2)], axis=1))
    last = []
    for q in range(2):
        for s in range(2):
            both = children[q][s] @ evaluate
            swapped = np.concatenate([both[:, PTS:], both[:, :PTS]], axis=1)
            last.append(three_parts(np.concatenate([both, swapped], axis=1)))
    return jnp.asarray(spread), jnp.asarray(np.stack(last))


def split_parts(value):
    high = value.astype(BF16)
    low = (value - high.astype(F32)).astype(BF16)
    return high, low


def sine_cosine(angle):
    u = angle * 0.5
    w = u * u
    s = -2.5052108e-08
    for c in (2.7557319e-06, -1.9841270e-04, 8.3333333e-03, -1.6666667e-01, 1.0):
        s = s * w + c
    s = s * u
    c_ = 2.0876757e-09
    for c in (-2.7557319e-07, 2.4801587e-05, -1.3888889e-03, 4.1666667e-02, -0.5, 1.0):
        c_ = c_ * w + c
    return 2.0 * s * c_, 1.0 - 2.0 * s * s


def swap(value):
    return pltpu.roll(value, PTS, value.ndim - 1)


def turn_tables(angle, before):
    sine, cosine = sine_cosine(angle)
    lane = lax.broadcasted_iota(jnp.int32, angle.shape, angle.ndim - 1)
    low = lane < PTS
    cos_swap, sin_swap = swap(cosine), swap(sine)
    cos = (jnp.where(low, cosine, cos_swap), jnp.where(low, cos_swap, cosine))
    if before:
        sin = (jnp.where(low, sine, -sin_swap), jnp.where(low, sin_swap, -sine))
    else:
        sin = (jnp.where(low, -sine, sin_swap), jnp.where(low, -sin_swap, sine))
    return cos, sin


def wait_for(ref, sem):
    pltpu.make_async_copy(ref, ref, sem).wait()


def butterfly_kernel(
    coeffs, phases, field_phases, w_all, w_last, out,
    cbuf, lpv, fpv, w_ref, wf_ref, cos1, sin1, cos_f, sin_f,
    send_a, recv_xa, send_ya, recv_ya, send_yb, recv_yb, recv_xb,
    pk, p1, pq, phs, cos_t, sin_t, xs, res, s4, r1, gz, gy, done,
    load_sem, out_sem, x_send, x_recv, in_send, in_recv, s1_send, s1_recv, s2_send, s2_recv, ph_send, ph_recv,
):
    big_x = lax.axis_index("qx")
    big_y = lax.axis_index("qy")
    z, core = big_x // 2, big_x % 2
    y, x = big_y // 4, big_y % 4
    pick = (z // 2) * 2 + y // 2

    loads = [
        pltpu.make_async_copy(src, dst, load_sem.at[n])
        for n, (src, dst) in enumerate(
            [
                (phases, lpv),
                (coeffs.at[:, 0], cbuf.at[0]),
                (coeffs.at[:, 1], cbuf.at[1]),
                (w_all, w_ref),
                (field_phases, fpv),
                (w_last.at[pick], wf_ref),
            ]
        )
    ]
    for load in loads:
        load.start()

    zs = [(z + d) % 4 for d in range(4)]
    cs = [core, 1 - core]
    ys = [(y + d) % 4 for d in range(4)]
    xs_ = [(x + d) % 4 for d in range(4)]
    y_odd = [(y + d) % 2 for d in range(4)]
    z_odd = [(z + d) % 2 for d in range(4)]
    dev_x = [[zs[dz] * 2 + cs[dc] for dc in range(2)] for dz in range(4)]
    dev_y = [[ys[dy] * 4 + xs_[dx] for dx in range(4)] for dy in range(4)]

    barrier = pltpu.get_barrier_semaphore()
    greeted = 0
    for dz in range(4):
        for dc in range(2):
            for dy in range(4):
                for dx in range(4):
                    if (dz, dc, dy, dx) != (0, 0, 0, 0) and 0 in (dz, dy, dx):
                        pl.semaphore_signal(
                            barrier, inc=1, device_id=(dev_x[dz][dc], dev_y[dy][dx]), device_id_type=MESH
                        )
                        greeted += 1

    def send(src, dst, send_sem, recv_sem, target):
        pltpu.make_async_remote_copy(
            src_ref=src, dst_ref=dst, send_sem=send_sem, recv_sem=recv_sem,
            device_id=target, device_id_type=MESH,
        ).start()

    me_in = big_x * 4 + y
    me_z = core * 16 + y * 4 + x
    me_y = big_x * 4 + x

    loads[0].wait()

    def first_tables(i, carry):
        some = pl.ds(i * 8, 8)
        cos, sin = turn_tables(lpv[some], True)
        for k in range(2):
            cos1[k, some] = cos[k]
            sin1[k, some] = sin[k]
        return carry

    lax.fori_loop(0, 16, first_tables, 0)

    def rotate_first(c):
        left, half = c // 2, c % 2
        if half == 0:
            loads[1 + left].wait()

        def step(j, carry):
            for n in range(16):
                i = j * 4 + n // 4
                vx = n % 4
                box = j * 16 + n
                direct = None
                crossed = None
                for k in range(2):
                    value = cbuf[left, box, k, pl.ds(half * 8, 8), :]
                    d = value * cos1[k, box, pl.ds(left, 1), :]
                    e = value * sin1[k, box, pl.ds(left, 1), :]
                    direct = d if direct is None else direct + d
                    crossed = e if crossed is None else crossed + e
                if left == 0:
                    send_a[half, vx, i] = direct + swap(crossed)
                else:
                    send_yb[half, i, vx] = direct + swap(crossed)
            return carry

        lax.fori_loop(0, 8, step, 0)

    def send_x(src, dst, send_sem, recv_sem):
        for dx in range(1, 4):
            send(src(xs_[dx]), dst, send_sem, recv_sem, (big_x, dev_y[0][dx]))

    def send_in(src, dst, send_sem, recv_sem):
        for d in range(1, 32):
            there_x = dev_x[d // 8][(d // 4) % 2]
            send(src(there_x * 4 + ys[d % 4]), dst, send_sem, recv_sem, (there_x, dev_y[d % 4][0]))

    def enter(c):
        h = c % 2
        if c < 2:
            send_x(lambda t: send_a.at[h, t], recv_xa.at[h, x], x_send.at[c], x_recv.at[c])
        else:
            send_in(lambda t: send_yb.at[h, t], recv_yb.at[h, me_in], in_send.at[c], in_recv.at[c])

    def pass_on(c):
        h = c % 2
        if c < 2:
            wait_for(recv_xa.at[h, pl.ds(0, 3)], x_recv.at[c])
            recv_xa[h, x] = send_a[h, x]

            def add(j, carry):
                some = pl.ds(j * 8, 8)
                for y1 in range(2):
                    send_ya[h, some, y1] = recv_xa[h, 2 * y1, some] + recv_xa[h, 2 * y1 + 1, some]
                return carry

            lax.fori_loop(0, 4, add, 0)
            send_in(lambda t: send_ya.at[h, t], recv_ya.at[h, me_in], in_send.at[c], in_recv.at[c])
            recv_ya[h, me_in] = send_ya[h, me_in]
        else:
            wait_for(recv_yb.at[h, pl.ds(0, 31)], in_recv.at[c])
            recv_yb[h, me_in] = send_yb[h, me_in]
            send_x(lambda t: recv_yb.at[h, :, t], recv_xb.at[h, x], x_send.at[c], x_recv.at[c])
            recv_xb[h, x] = recv_yb[h, :, x]

    spans = (pl.ds(0, 1), pl.ds(1, 2))

    def pack_phases(j, carry):
        for n in range(4):
            i = j * 4 + n
            for level in range(3):
                for vx in range(4):
                    pk[i, level, 2 * vx : 2 * vx + 2] = lpv[i * 4 + vx, 2 * level + 2 : 2 * level + 4]
        return carry

    def send_phases(part):
        span = spans[part]
        send_in(lambda t: pk.at[t, span], p1.at[me_in, span], ph_send.at[part], ph_recv.at[part])
        p1[me_in, span] = pk[me_in, span]

    def pass_phases(part):
        span = spans[part]
        wait_for(p1.at[pl.ds(0, 31), span], ph_recv.at[part])

        def pack(i, carry):
            for level in (0,) if part == 0 else (1, 2):
                for sx in range(4):
                    for sy in range(4):
                        pq[sx, level, i, 2 * sy : 2 * sy + 2] = p1[i * 4 + sy, level, 2 * sx : 2 * sx + 2]
            return carry

        lax.fori_loop(0, 8, pack, 0)
        send_x(lambda t: pq.at[t, span], phs.at[x, span], ph_send.at[2 + part], ph_recv.at[2 + part])
        phs[x, span] = pq[x, span]

    def phase_tables(part):
        span = spans[part]
        wait_for(phs.at[pl.ds(0, 3), span], ph_recv.at[2 + part])

        def table(sx, carry):
            for level in (0,) if part == 0 else (1, 2):
                cos, sin = turn_tables(phs[sx, level], True)
                for k in range(2):
                    cos_t[level, k, sx] = cos[k]
                    sin_t[level, k, sx] = sin[k]
            return carry

        lax.fori_loop(0, 4, table, 0)

    def field_tables():
        loads[4].wait()

        def table(i, carry):
            cos, sin = turn_tables(fpv[i], False)
            for k in range(2):
                cos_f[k, i] = cos[k]
                sin_f[k, i] = sin[k]
            return carry

        lax.fori_loop(0, 8, table, 0)

    def put_parts(row, value):
        high, low = split_parts(value)
        rows = pl.ds(pl.multiple_of(row, 16), 16)
        xs[rows, 0:WIDE] = high
        xs[rows, WIDE : 2 * WIDE] = low
        xs[rows, 2 * WIDE : 3 * WIDE] = high

    def multiply():
        res[...] = jnp.dot(xs[...], w_ref[...], preferred_element_type=F32)

    def turned_sum(parts, level, left):
        direct = None
        crossed = None
        for block, column, k, at_x, at_y, at_v in parts:
            value = res[pl.ds(pl.multiple_of(block * 8, 8), 8), column * WIDE : (column + 1) * WIDE]
            row = pl.ds(2 * at_y + left, 1)
            d = value * cos_t[level, k, at_v, at_x, row, :]
            e = value * sin_t[level, k, at_v, at_x, row, :]
            direct = d if direct is None else direct + d
            crossed = e if crossed is None else crossed + e
        return direct + swap(crossed)

    def level_one(c):
        h = c % 2
        if c < 2:
            wait_for(recv_ya.at[h, pl.ds(0, 31)], in_recv.at[c])
        else:
            wait_for(recv_xb.at[h, pl.ds(0, 3)], x_recv.at[c])

        def first(j, carry):
            for n in range(8):
                i = j * 8 + n
                if c < 2:
                    value = recv_ya[h, i].reshape(16, WIDE)
                else:
                    value = jnp.concatenate(
                        [recv_xb[h, 2 * y1, i] + recv_xb[h, 2 * y1 + 1, i] for y1 in range(2)], axis=0
                    )
                put_parts(i * 16, value)
            return carry

        lax.fori_loop(0, 4, first, 0)
        multiply()

    def level_two(c):
        left = c // 2

        def second(a, carry):
            for y3, y2, y0 in DIGITS:
                outs = []
                for k in range(2):
                    parts = []
                    for x0 in range(2):
                        for y1 in range(2):
                            block = a * 16 + (x0 * 8 + y3 * 4 + y2 * 2 + y1)
                            parts.append((block, k * 2 + y0, k, a * 2 + x0, y3 * 2 + y2, y1 * 2 + y0))
                    outs.append(turned_sum(parts, 0, left))
                put_parts(a * 128 + (y3 * 4 + y2 * 2 + y0) * 16, jnp.concatenate(outs, axis=0))
            return carry

        lax.fori_loop(0, 4, second, 0)
        multiply()

    def other_levels(c):
        left = c // 2

        def third(x2, carry):
            for y3, y0, k in DIGITS:
                for x0 in range(2):
                    outs = []
                    for y1 in range(2):
                        parts = []
                        for x1 in range(2):
                            for y2 in range(2):
                                block = x2 * 32 + (x1 * 16 + y3 * 8 + y2 * 4 + y0 * 2 + k)
                                at_x = x2 * 4 + (x1 * 2 + x0)
                                parts.append((block, x0 * 2 + y1, k, at_x, y3 * 2 + y2, y1 * 2 + y0))
                        outs.append(turned_sum(parts, 1, left))
                    put_parts(
                        x2 * 256 + (y3 * 8 + y0 * 4 + k * 2 + x0) * 16, jnp.concatenate(outs, axis=0)
                    )
            return carry

        lax.fori_loop(0, 2, third, 0)
        multiply()

        def fourth(y0, carry):
            for k, x0, y1 in DIGITS:
                for x1 in range(2):
                    for y2 in range(2):
                        parts = []
                        for x2 in range(2):
                            for y3 in range(2):
                                block = y0 * 8 + (x2 * 32 + y3 * 16 + k * 4 + x0 * 2 + y1)
                                at_x = x2 * 4 + x1 * 2 + x0
                                parts.append((block, x1 * 2 + y2, k, at_x, y3 * 2 + y2, y1 * 2 + y0))
                        if k == 0:
                            s4[c, 0, y0 + (x0 * 8 + y2 * 4 + y1 * 2), x1] = turned_sum(parts, 2, left)
                        else:
                            s4[c, 1, y0 + (x1 * 8 + x0 * 4 + y1 * 2), y2] = turned_sum(parts, 2, left)
            return carry

        lax.fori_loop(0, 2, fourth, 0)

        for d in range(1, 32):
            dc, dt, dx = d // 16, (d // 4) % 4, d % 4
            send(
                s4.at[c, 0, cs[dc] * 8 + y_odd[dt] * 4 + xs_[dx]], r1.at[c, 0, me_z],
                s1_send.at[c, 0], s1_recv.at[c, 0], (dev_x[0][dc], dev_y[dt][dx]),
            )
            send(
                s4.at[c, 1, z_odd[dt] * 8 + cs[dc] * 4 + xs_[dx]], r1.at[c, 1, me_y],
                s1_send.at[c, 1], s1_recv.at[c, 1], (dev_x[dt][dc], dev_y[0][dx]),
            )
        r1[c, 0, me_z] = s4[c, 0, core * 8 + y_odd[0] * 4 + x]
        r1[c, 1, me_y] = s4[c, 1, z_odd[0] * 8 + core * 4 + x]

    def out_last(c, k):
        wait_for(r1.at[c, k, pl.ds(0, 31)], s1_recv.at[c, k])
        for d in (2, 1, 3):
            if k == 0:
                send(
                    r1.at[c, 0, :, z_odd[d]], gz.at[c, z], s2_send.at[c, 0], s2_recv.at[c, 0],
                    (dev_x[d][0], big_y),
                )
            else:
                send(
                    r1.at[c, 1, :, y_odd[d]], gy.at[c, y], s2_send.at[c, 1], s2_recv.at[c, 1],
                    (big_x, dev_y[d][0]),
                )
        if k == 0:
            gz[c, z] = r1[c, 0, :, z_odd[0]]
        else:
            gy[c, y] = r1[c, 1, :, y_odd[0]]

    def finish(c, k):
        left, half = c // 2, c % 2
        got = gz if k == 0 else gy
        wait_for(got.at[c, pl.ds(0, 3)], s2_recv.at[c, k])

        def piece(p, carry):
            for a in range(2):
                for n in range(16):
                    put_parts((a * 16 + n) * 16, got[c, p * 2 + a, pl.ds(2 * n, 2)].reshape(16, WIDE))
            res[:, 0 : 2 * WIDE] = jnp.dot(xs[...], wf_ref[...], preferred_element_type=F32)
            for a in range(2):
                for n in range(32):
                    if k == 0:
                        box_h, box_v = p * 4 + (a * 2 + n // 16), n % 16
                    else:
                        box_h, box_v = n // 4, p * 8 + (a * 4 + n % 4)
                    rows = slice((a * 32 + n) * 8, (a * 32 + n + 1) * 8)
                    at = pl.ds(box_v * 2 + left, 1)
                    done[c, k, box_h * 16 + box_v] = (
                        res[rows, 0:WIDE] * cos_f[k, box_h, at, :]
                        + res[rows, WIDE : 2 * WIDE] * sin_f[k, box_h, at, :]
                    )
            return carry

        lax.fori_loop(0, 2, piece, 0)
        store = pltpu.make_async_copy(
            done.at[c, k], out.at[:, left, k, pl.ds(half * 8, 8)], out_sem.at[c, k]
        )
        store.start()
        stores.append(store)

    stores = []
    lax.fori_loop(0, 8, pack_phases, 0)
    rotate_first(0)
    pl.semaphore_wait(barrier, greeted)
    enter(0)
    send_phases(0)
    send_phases(1)
    rotate_first(1)
    enter(1)
    rotate_first(2)
    enter(2)
    pass_phases(0)
    pass_on(0)
    pass_phases(1)
    rotate_first(3)
    enter(3)
    pass_on(2)
    pass_on(1)
    loads[3].wait()
    field_tables()
    phase_tables(0)
    level_one(0)
    level_two(0)
    phase_tables(1)
    other_levels(0)
    pass_on(3)
    level_one(2)
    level_two(2)
    other_levels(2)
    level_one(1)
    out_last(0, 0)
    out_last(0, 1)
    level_two(1)
    other_levels(1)
    out_last(2, 0)
    level_one(3)
    level_two(3)
    out_last(2, 1)
    other_levels(3)
    out_last(1, 1)
    out_last(1, 0)
    loads[5].wait()
    finish(0, 0)
    finish(0, 1)
    out_last(3, 1)
    out_last(3, 0)
    for c in (2, 1, 3):
        finish(c, 0)
        finish(c, 1)
    for c in range(4):
        h = c % 2
        wait_for(recv_xa.at[h, pl.ds(0, 3)], x_send.at[c])
        wait_for((recv_ya if c < 2 else recv_yb).at[h, pl.ds(0, 31)], in_send.at[c])
        for k in range(2):
            wait_for(r1.at[c, k, pl.ds(0, 31)], s1_send.at[c, k])
            wait_for(gz.at[c, pl.ds(0, 3)], s2_send.at[c, k])
    for store in stores:
        store.wait()
    for part in range(2):
        wait_for(p1.at[pl.ds(0, 31), spans[part]], ph_send.at[part])
        wait_for(phs.at[pl.ds(0, 3), spans[part]], ph_send.at[2 + part])


def butterfly(coeffs, phases, field_phases, spread, last):
    dma = pltpu.SemaphoreType.DMA
    tile = (8, WIDE)

    def vmem(*shape):
        return pltpu.VMEM(shape + tile, F32)

    return pl.pallas_call(
        butterfly_kernel,
        out_shape=jax.ShapeDtypeStruct((128, 2, 2, 16, WIDE), F32),
        in_specs=[pl.BlockSpec(memory_space=pltpu.HBM)] * 5,
        out_specs=pl.BlockSpec(memory_space=pltpu.HBM),
        scratch_shapes=[
            pltpu.VMEM((2, 128, 2, 16, WIDE), F32),
            vmem(128),
            pltpu.VMEM((8, 32, WIDE), F32),
            pltpu.VMEM((3 * WIDE, 4 * WIDE), BF16),
            pltpu.VMEM((3 * WIDE, 2 * WIDE), BF16),
            vmem(2, 128),
            vmem(2, 128),
            pltpu.VMEM((2, 8, 32, WIDE), F32),
            pltpu.VMEM((2, 8, 32, WIDE), F32),
            vmem(2, 4, 32),
            vmem(2, 4, 32),
            vmem(2, 32, 2),
            vmem(2, 32, 2),
            vmem(2, 32, 4),
            vmem(2, 32, 4),
            vmem(2, 4, 32),
            vmem(32, 3),
            vmem(32, 3),
            vmem(4, 3, 8),
            vmem(4, 3, 8),
            vmem(3, 2, 4, 8),
            vmem(3, 2, 4, 8),
            pltpu.VMEM((512, 3 * WIDE), BF16),
            pltpu.VMEM((512, 4 * WIDE), F32),
            vmem(4, 2, 16, 2),
            vmem(4, 2, 32, 2),
            vmem(4, 4, 32),
            vmem(4, 4, 32),
            vmem(4, 2, 128),
            dma((6,)),
            dma((4, 2)),
            dma((4,)),
            dma((4,)),
            dma((4,)),
            dma((4,)),
            dma((4, 2)),
            dma((4, 2)),
            dma((4, 2)),
            dma((4, 2)),
            dma((4,)),
            dma((4,)),
        ],
        compiler_params=pltpu.CompilerParams(
            collective_id=0, has_side_effects=True, vmem_limit_bytes=60 * 2**20
        ),
        name="butterfly",
    )(coeffs, phases, field_phases, spread, last)


def hand_on_kernel(done, out, held, in_sem, out_sem):
    parts = in_sem.shape[0]
    rows = done.shape[0] // parts
    into, onto = [], []
    for n in range(parts):
        some = pl.ds(n * rows, rows)
        into.append(pltpu.make_async_copy(done.at[some], held.at[some], in_sem.at[n]))
        onto.append(pltpu.make_async_copy(held.at[some], out.at[some], out_sem.at[n]))
        into[n].start()
    for n in range(parts):
        into[n].wait()
        onto[n].start()
    for n in range(parts):
        onto[n].wait()


def hand_on(done, parts=4):
    return pl.pallas_call(
        hand_on_kernel,
        out_shape=jax.ShapeDtypeStruct(done.shape, F32),
        in_specs=[pl.BlockSpec(memory_space=pltpu.HBM)],
        out_specs=pl.BlockSpec(memory_space=pltpu.HBM),
        scratch_shapes=[
            pltpu.VMEM(done.shape, F32),
            pltpu.SemaphoreType.DMA((parts,)),
            pltpu.SemaphoreType.DMA((parts,)),
        ],
        compiler_params=pltpu.CompilerParams(vmem_limit_bytes=60 * 2**20),
        name="hand_on",
    )(done)


def per_device(coeffs, level_phase, field_phase):
    spread, last = weights()
    done = butterfly(
        coeffs.reshape(128, 2, 2, 16, WIDE), level_phase.reshape(128, 8, WIDE),
        field_phase.reshape(8, 32, WIDE), spread, last,
    )
    return hand_on(done).reshape(coeffs.shape)


def solution(mesh):
    return jax.shard_map(
        per_device,
        mesh=mesh,
        in_specs=(
            P("qx", "qy", None, None, None, None, None, None),
            P("qx", "qy", None, None, None, None, None),
            P("qx", "qy", None, None, None, None),
        ),
        out_specs=P("qx", "qy", None, None, None, None, None, None),
        check_vma=False,
    )
```

```python
import functools

import jax
import jax.numpy as jnp
import numpy as np
from jax import lax
from jax.experimental import pallas as pl
from jax.experimental.pallas import tpu as pltpu
from jax.sharding import PartitionSpec as P

CHEB = 8
PTS = CHEB * CHEB
WIDE = 2 * PTS
MESH = pl.DeviceIdType.MESH
F32 = jnp.float32
BF16 = jnp.bfloat16
DIGITS = [(a, b, c) for a in range(2) for b in range(2) for c in range(2)]


def point_tables(count):
    points = 0.5 - 0.5 * np.cos((2 * np.arange(count) + 1) * np.pi / (2 * count))

    def lagrange(places):
        values = np.ones((len(places), count))
        for k in range(count):
            for m in range(count):
                if m != k:
                    values[:, k] = values[:, k] * (places - points[m]) / (points[k] - points[m])
        return values

    halves = [lagrange((q + points) / 2.0) for q in range(2)]
    uniform = lagrange((np.arange(count) + 0.5) / count)
    identity = np.eye(2)
    children = [
        [np.kron(identity, np.kron(halves[q], halves[s])).T for s in range(2)] for q in range(2)
    ]
    evaluate = np.kron(identity, np.kron(uniform, uniform)).T
    return children, evaluate


def three_parts(matrix):
    high = matrix.astype(np.float32).astype(BF16)
    low = (matrix - high.astype(np.float64)).astype(np.float32).astype(BF16)
    return np.concatenate([high, high, low], axis=0)


def weights():
    children, evaluate = point_tables(CHEB)
    spread = three_parts(np.concatenate([children[q][s] for q in range(2) for s in range(2)], axis=1))
    last = []
    for q in range(2):
        for s in range(2):
            both = children[q][s] @ evaluate
            swapped = np.concatenate([both[:, PTS:], both[:, :PTS]], axis=1)
            last.append(three_parts(np.concatenate([both, swapped], axis=1)))
    return jnp.asarray(spread), jnp.asarray(np.stack(last))


def split_parts(value):
    high = value.astype(BF16)
    low = (value - high.astype(F32)).astype(BF16)
    return high, low


def sine_cosine(angle):
    u = angle * 0.5
    w = u * u
    s = -2.5052108e-08
    for c in (2.7557319e-06, -1.9841270e-04, 8.3333333e-03, -1.6666667e-01, 1.0):
        s = s * w + c
    s = s * u
    c_ = 2.0876757e-09
    for c in (-2.7557319e-07, 2.4801587e-05, -1.3888889e-03, 4.1666667e-02, -0.5, 1.0):
        c_ = c_ * w + c
    return 2.0 * s * c_, 1.0 - 2.0 * s * s


def swap(value):
    return pltpu.roll(value, PTS, value.ndim - 1)


def turn_tables(angle, before):
    sine, cosine = sine_cosine(angle)
    lane = lax.broadcasted_iota(jnp.int32, angle.shape, angle.ndim - 1)
    low = lane < PTS
    cos_swap, sin_swap = swap(cosine), swap(sine)
    cos = (jnp.where(low, cosine, cos_swap), jnp.where(low, cos_swap, cosine))
    if before:
        sin = (jnp.where(low, sine, -sin_swap), jnp.where(low, sin_swap, -sine))
    else:
        sin = (jnp.where(low, -sine, sin_swap), jnp.where(low, -sin_swap, sine))
    return cos, sin


def place_parts(xs, row, value):
    high, low = split_parts(value)
    rows = pl.ds(pl.multiple_of(row, 16), 16)
    xs[rows, 0:WIDE] = high
    xs[rows, WIDE : 2 * WIDE] = low
    xs[rows, 2 * WIDE : 3 * WIDE] = high


def last_stage(got, put, k, left, xs, res, wf_ref, cos_f, sin_f):
    def piece(p, carry):
        for a in range(2):
            for n in range(16):
                place_parts(xs, (a * 16 + n) * 16, got[p * 2 + a, pl.ds(2 * n, 2)].reshape(16, WIDE))
        res[:, 0 : 2 * WIDE] = jnp.dot(xs[...], wf_ref[...], preferred_element_type=F32)
        for a in range(2):
            for n in range(32):
                if k == 0:
                    box_h, box_v = p * 4 + (a * 2 + n // 16), n % 16
                else:
                    box_h, box_v = n // 4, p * 8 + (a * 4 + n % 4)
                rows = slice((a * 32 + n) * 8, (a * 32 + n + 1) * 8)
                at = pl.ds(box_v * 2 + left, 1)
                put(
                    box_h * 16 + box_v,
                    res[rows, 0:WIDE] * cos_f[k, box_h, at, :]
                    + res[rows, WIDE : 2 * WIDE] * sin_f[k, box_h, at, :],
                )
        return carry

    lax.fori_loop(0, 2, piece, 0)


def field_turns(fpv, cos_f, sin_f):
    def table(i, carry):
        cos, sin = turn_tables(fpv[i], False)
        for k in range(2):
            cos_f[k, i] = cos[k]
            sin_f[k, i] = sin[k]
        return carry

    lax.fori_loop(0, 8, table, 0)


def wait_for(ref, sem):
    pltpu.make_async_copy(ref, ref, sem).wait()


def butterfly_kernel(
    coeffs, phases, field_phases, w_all, w_last, out, gz3, gy3,
    cbuf, lpv, fpv, w_ref, wf_ref, cos1, sin1, cos_f, sin_f,
    send_a, recv_xa, send_ya, recv_ya, send_yb, recv_yb, recv_xb,
    pk, p1, pq, phs, cos_t, sin_t, xs, res, s4, r1, gz, gy, done,
    load_sem, out_sem, own_sem, x_send, x_recv, in_send, in_recv, s1_send, s1_recv, s2_send, s2_recv, ph_send, ph_recv,
):
    big_x = lax.axis_index("qx")
    big_y = lax.axis_index("qy")
    z, core = big_x // 2, big_x % 2
    y, x = big_y // 4, big_y % 4
    pick = (z // 2) * 2 + y // 2

    loads = [
        pltpu.make_async_copy(src, dst, load_sem.at[n])
        for n, (src, dst) in enumerate(
            [
                (phases, lpv),
                (coeffs.at[:, 0], cbuf.at[0]),
                (coeffs.at[:, 1], cbuf.at[1]),
                (w_all, w_ref),
                (field_phases, fpv),
                (w_last.at[pick], wf_ref),
            ]
        )
    ]
    for load in loads:
        load.start()

    zs = [(z + d) % 4 for d in range(4)]
    cs = [core, 1 - core]
    ys = [(y + d) % 4 for d in range(4)]
    xs_ = [(x + d) % 4 for d in range(4)]
    y_odd = [(y + d) % 2 for d in range(4)]
    z_odd = [(z + d) % 2 for d in range(4)]
    dev_x = [[zs[dz] * 2 + cs[dc] for dc in range(2)] for dz in range(4)]
    dev_y = [[ys[dy] * 4 + xs_[dx] for dx in range(4)] for dy in range(4)]

    barrier = pltpu.get_barrier_semaphore()
    greeted = 0
    for dz in range(4):
        for dc in range(2):
            for dy in range(4):
                for dx in range(4):
                    if (dz, dc, dy, dx) != (0, 0, 0, 0) and 0 in (dz, dy, dx):
                        pl.semaphore_signal(
                            barrier, inc=1, device_id=(dev_x[dz][dc], dev_y[dy][dx]), device_id_type=MESH
                        )
                        greeted += 1

    def send(src, dst, send_sem, recv_sem, target):
        pltpu.make_async_remote_copy(
            src_ref=src, dst_ref=dst, send_sem=send_sem, recv_sem=recv_sem,
            device_id=target, device_id_type=MESH,
        ).start()

    me_in = big_x * 4 + y
    me_z = core * 16 + y * 4 + x
    me_y = big_x * 4 + x

    loads[0].wait()

    def first_tables(i, carry):
        some = pl.ds(i * 8, 8)
        cos, sin = turn_tables(lpv[some], True)
        for k in range(2):
            cos1[k, some] = cos[k]
            sin1[k, some] = sin[k]
        return carry

    lax.fori_loop(0, 16, first_tables, 0)

    def rotate_first(c):
        left, half = c // 2, c % 2
        if half == 0:
            loads[1 + left].wait()

        def step(j, carry):
            for n in range(16):
                i = j * 4 + n // 4
                vx = n % 4
                box = j * 16 + n
                direct = None
                crossed = None
                for k in range(2):
                    value = cbuf[left, box, k, pl.ds(half * 8, 8), :]
                    d = value * cos1[k, box, pl.ds(left, 1), :]
                    e = value * sin1[k, box, pl.ds(left, 1), :]
                    direct = d if direct is None else direct + d
                    crossed = e if crossed is None else crossed + e
                if left == 0:
                    send_a[half, vx, i] = direct + swap(crossed)
                else:
                    send_yb[half, i, vx] = direct + swap(crossed)
            return carry

        lax.fori_loop(0, 8, step, 0)

    def send_x(src, dst, send_sem, recv_sem):
        for dx in range(1, 4):
            send(src(xs_[dx]), dst, send_sem, recv_sem, (big_x, dev_y[0][dx]))

    def send_in(src, dst, send_sem, recv_sem):
        for d in range(1, 32):
            there_x = dev_x[d // 8][(d // 4) % 2]
            send(src(there_x * 4 + ys[d % 4]), dst, send_sem, recv_sem, (there_x, dev_y[d % 4][0]))

    def enter(c):
        h = c % 2
        if c < 2:
            send_x(lambda t: send_a.at[h, t], recv_xa.at[h, x], x_send.at[c], x_recv.at[c])
        else:
            send_in(lambda t: send_yb.at[h, t], recv_yb.at[h, me_in], in_send.at[c], in_recv.at[c])

    def pass_on(c):
        h = c % 2
        if c < 2:
            wait_for(recv_xa.at[h, pl.ds(0, 3)], x_recv.at[c])
            recv_xa[h, x] = send_a[h, x]

            def add(j, carry):
                some = pl.ds(j * 8, 8)
                for y1 in range(2):
                    send_ya[h, some, y1] = recv_xa[h, 2 * y1, some] + recv_xa[h, 2 * y1 + 1, some]
                return carry

            lax.fori_loop(0, 4, add, 0)
            send_in(lambda t: send_ya.at[h, t], recv_ya.at[h, me_in], in_send.at[c], in_recv.at[c])
            recv_ya[h, me_in] = send_ya[h, me_in]
        else:
            wait_for(recv_yb.at[h, pl.ds(0, 31)], in_recv.at[c])
            recv_yb[h, me_in] = send_yb[h, me_in]
            send_x(lambda t: recv_yb.at[h, :, t], recv_xb.at[h, x], x_send.at[c], x_recv.at[c])
            recv_xb[h, x] = recv_yb[h, :, x]

    spans = (pl.ds(0, 1), pl.ds(1, 2))

    def pack_phases(j, carry):
        for n in range(4):
            i = j * 4 + n
            for level in range(3):
                for vx in range(4):
                    pk[i, level, 2 * vx : 2 * vx + 2] = lpv[i * 4 + vx, 2 * level + 2 : 2 * level + 4]
        return carry

    def send_phases(part):
        span = spans[part]
        send_in(lambda t: pk.at[t, span], p1.at[me_in, span], ph_send.at[part], ph_recv.at[part])
        p1[me_in, span] = pk[me_in, span]

    def pass_phases(part):
        span = spans[part]
        wait_for(p1.at[pl.ds(0, 31), span], ph_recv.at[part])

        def pack(i, carry):
            for level in (0,) if part == 0 else (1, 2):
                for sx in range(4):
                    for sy in range(4):
                        pq[sx, level, i, 2 * sy : 2 * sy + 2] = p1[i * 4 + sy, level, 2 * sx : 2 * sx + 2]
            return carry

        lax.fori_loop(0, 8, pack, 0)
        send_x(lambda t: pq.at[t, span], phs.at[x, span], ph_send.at[2 + part], ph_recv.at[2 + part])
        phs[x, span] = pq[x, span]

    def phase_tables(part):
        span = spans[part]
        wait_for(phs.at[pl.ds(0, 3), span], ph_recv.at[2 + part])

        def table(sx, carry):
            for level in (0,) if part == 0 else (1, 2):
                cos, sin = turn_tables(phs[sx, level], True)
                for k in range(2):
                    cos_t[level, k, sx] = cos[k]
                    sin_t[level, k, sx] = sin[k]
            return carry

        lax.fori_loop(0, 4, table, 0)

    def field_tables():
        loads[4].wait()
        field_turns(fpv, cos_f, sin_f)

    def put_parts(row, value):
        place_parts(xs, row, value)

    def multiply():
        res[...] = jnp.dot(xs[...], w_ref[...], preferred_element_type=F32)

    def turned_sum(parts, level, left):
        direct = None
        crossed = None
        for block, column, k, at_x, at_y, at_v in parts:
            value = res[pl.ds(pl.multiple_of(block * 8, 8), 8), column * WIDE : (column + 1) * WIDE]
            row = pl.ds(2 * at_y + left, 1)
            d = value * cos_t[level, k, at_v, at_x, row, :]
            e = value * sin_t[level, k, at_v, at_x, row, :]
            direct = d if direct is None else direct + d
            crossed = e if crossed is None else crossed + e
        return direct + swap(crossed)

    def level_one(c):
        h = c % 2
        if c < 2:
            wait_for(recv_ya.at[h, pl.ds(0, 31)], in_recv.at[c])
        else:
            wait_for(recv_xb.at[h, pl.ds(0, 3)], x_recv.at[c])

        def first(j, carry):
            for n in range(8):
                i = j * 8 + n
                if c < 2:
                    value = recv_ya[h, i].reshape(16, WIDE)
                else:
                    value = jnp.concatenate(
                        [recv_xb[h, 2 * y1, i] + recv_xb[h, 2 * y1 + 1, i] for y1 in range(2)], axis=0
                    )
                put_parts(i * 16, value)
            return carry

        lax.fori_loop(0, 4, first, 0)
        multiply()

    def level_two(c):
        left = c // 2

        def second(a, carry):
            for y3, y2, y0 in DIGITS:
                outs = []
                for k in range(2):
                    parts = []
                    for x0 in range(2):
                        for y1 in range(2):
                            block = a * 16 + (x0 * 8 + y3 * 4 + y2 * 2 + y1)
                            parts.append((block, k * 2 + y0, k, a * 2 + x0, y3 * 2 + y2, y1 * 2 + y0))
                    outs.append(turned_sum(parts, 0, left))
                put_parts(a * 128 + (y3 * 4 + y2 * 2 + y0) * 16, jnp.concatenate(outs, axis=0))
            return carry

        lax.fori_loop(0, 4, second, 0)
        multiply()

    def other_levels(c):
        left = c // 2

        def third(x2, carry):
            for y3, y0, k in DIGITS:
                for x0 in range(2):
                    outs = []
                    for y1 in range(2):
                        parts = []
                        for x1 in range(2):
                            for y2 in range(2):
                                block = x2 * 32 + (x1 * 16 + y3 * 8 + y2 * 4 + y0 * 2 + k)
                                at_x = x2 * 4 + (x1 * 2 + x0)
                                parts.append((block, x0 * 2 + y1, k, at_x, y3 * 2 + y2, y1 * 2 + y0))
                        outs.append(turned_sum(parts, 1, left))
                    put_parts(
                        x2 * 256 + (y3 * 8 + y0 * 4 + k * 2 + x0) * 16, jnp.concatenate(outs, axis=0)
                    )
            return carry

        lax.fori_loop(0, 2, third, 0)
        multiply()

        def fourth(y0, carry):
            for k, x0, y1 in DIGITS:
                for x1 in range(2):
                    for y2 in range(2):
                        parts = []
                        for x2 in range(2):
                            for y3 in range(2):
                                block = y0 * 8 + (x2 * 32 + y3 * 16 + k * 4 + x0 * 2 + y1)
                                at_x = x2 * 4 + x1 * 2 + x0
                                parts.append((block, x1 * 2 + y2, k, at_x, y3 * 2 + y2, y1 * 2 + y0))
                        if k == 0:
                            s4[c, 0, y0 + (x0 * 8 + y2 * 4 + y1 * 2), x1] = turned_sum(parts, 2, left)
                        else:
                            s4[c, 1, y0 + (x1 * 8 + x0 * 4 + y1 * 2), y2] = turned_sum(parts, 2, left)
            return carry

        lax.fori_loop(0, 2, fourth, 0)

        for d in range(1, 32):
            dc, dt, dx = d // 16, (d // 4) % 4, d % 4
            send(
                s4.at[c, 0, cs[dc] * 8 + y_odd[dt] * 4 + xs_[dx]], r1.at[c, 0, me_z],
                s1_send.at[c, 0], s1_recv.at[c, 0], (dev_x[0][dc], dev_y[dt][dx]),
            )
            send(
                s4.at[c, 1, z_odd[dt] * 8 + cs[dc] * 4 + xs_[dx]], r1.at[c, 1, me_y],
                s1_send.at[c, 1], s1_recv.at[c, 1], (dev_x[dt][dc], dev_y[0][dx]),
            )
        r1[c, 0, me_z] = s4[c, 0, core * 8 + y_odd[0] * 4 + x]
        r1[c, 1, me_y] = s4[c, 1, z_odd[0] * 8 + core * 4 + x]

    def out_last(c, k):
        wait_for(r1.at[c, k, pl.ds(0, 31)], s1_recv.at[c, k])
        to_z, to_y = (gz3, gy3) if c == 3 else (gz.at[c], gy.at[c])
        for d in (2, 1, 3):
            if k == 0:
                send(
                    r1.at[c, 0, :, z_odd[d]], to_z.at[z], s2_send.at[c, 0], s2_recv.at[c, 0],
                    (dev_x[d][0], big_y),
                )
            else:
                send(
                    r1.at[c, 1, :, y_odd[d]], to_y.at[y], s2_send.at[c, 1], s2_recv.at[c, 1],
                    (big_x, dev_y[d][0]),
                )
        if c == 3:
            kept.append(
                pltpu.make_async_copy(r1.at[c, 0, :, z_odd[0]], gz3.at[z], own_sem.at[0])
                if k == 0
                else pltpu.make_async_copy(r1.at[c, 1, :, y_odd[0]], gy3.at[y], own_sem.at[1])
            )
            kept[-1].start()
        elif k == 0:
            gz[c, z] = r1[c, 0, :, z_odd[0]]
        else:
            gy[c, y] = r1[c, 1, :, y_odd[0]]

    def finish(c, k):
        left, half = c // 2, c % 2
        got = gz if k == 0 else gy
        wait_for(got.at[c, pl.ds(0, 3)], s2_recv.at[c, k])

        def put(place, value):
            done[c, k, place] = value

        last_stage(got.at[c], put, k, left, xs, res, wf_ref, cos_f, sin_f)
        store = pltpu.make_async_copy(
            done.at[c, k], out.at[:, left, k, pl.ds(half * 8, 8)], out_sem.at[c, k]
        )
        store.start()
        stores.append(store)

    stores = []
    kept = []
    lax.fori_loop(0, 8, pack_phases, 0)
    rotate_first(0)
    pl.semaphore_wait(barrier, greeted)
    enter(0)
    send_phases(0)
    send_phases(1)
    rotate_first(2)
    enter(2)
    rotate_first(1)
    enter(1)
    pass_phases(0)
    pass_phases(1)
    pass_on(0)
    pass_on(2)
    pass_on(1)
    rotate_first(3)
    enter(3)
    loads[3].wait()
    field_tables()
    level_one(0)
    phase_tables(0)
    level_two(0)
    phase_tables(1)
    other_levels(0)
    level_one(1)
    level_two(1)
    other_levels(1)
    out_last(0, 0)
    pass_on(3)
    level_one(2)
    out_last(0, 1)
    out_last(1, 0)
    out_last(1, 1)
    level_two(2)
    other_levels(2)
    level_one(3)
    level_two(3)
    other_levels(3)
    out_last(2, 0)
    out_last(2, 1)
    loads[5].wait()
    finish(0, 0)
    out_last(3, 1)
    finish(1, 0)
    out_last(3, 0)
    finish(0, 1)
    finish(1, 1)
    finish(2, 0)
    finish(2, 1)
    wait_for(gz3.at[pl.ds(0, 3)], s2_recv.at[3, 0])
    wait_for(gy3.at[pl.ds(0, 3)], s2_recv.at[3, 1])
    for c in range(4):
        h = c % 2
        wait_for(recv_xa.at[h, pl.ds(0, 3)], x_send.at[c])
        wait_for((recv_ya if c < 2 else recv_yb).at[h, pl.ds(0, 31)], in_send.at[c])
        for k in range(2):
            wait_for(r1.at[c, k, pl.ds(0, 31)], s1_send.at[c, k])
            wait_for(gz.at[0, pl.ds(0, 3)], s2_send.at[c, k])
    for store in stores + kept:
        store.wait()
    for part in range(2):
        wait_for(p1.at[pl.ds(0, 31), spans[part]], ph_send.at[part])
        wait_for(phs.at[pl.ds(0, 3), spans[part]], ph_send.at[2 + part])


def butterfly(coeffs, phases, field_phases, spread, last):
    dma = pltpu.SemaphoreType.DMA
    tile = (8, WIDE)

    def vmem(*shape):
        return pltpu.VMEM(shape + tile, F32)

    return pl.pallas_call(
        butterfly_kernel,
        out_shape=(
            jax.ShapeDtypeStruct((128, 2, 2, 16, WIDE), F32),
            jax.ShapeDtypeStruct((4, 32) + tile, F32),
            jax.ShapeDtypeStruct((4, 32) + tile, F32),
        ),
        in_specs=[pl.BlockSpec(memory_space=pltpu.HBM)] * 5,
        out_specs=tuple(pl.BlockSpec(memory_space=pltpu.HBM) for _ in range(3)),
        scratch_shapes=[
            pltpu.VMEM((2, 128, 2, 16, WIDE), F32),
            vmem(128),
            pltpu.VMEM((8, 32, WIDE), F32),
            pltpu.VMEM((3 * WIDE, 4 * WIDE), BF16),
            pltpu.VMEM((3 * WIDE, 2 * WIDE), BF16),
            vmem(2, 128),
            vmem(2, 128),
            pltpu.VMEM((2, 8, 32, WIDE), F32),
            pltpu.VMEM((2, 8, 32, WIDE), F32),
            vmem(2, 4, 32),
            vmem(2, 4, 32),
            vmem(2, 32, 2),
            vmem(2, 32, 2),
            vmem(2, 32, 4),
            vmem(2, 32, 4),
            vmem(2, 4, 32),
            vmem(32, 3),
            vmem(32, 3),
            vmem(4, 3, 8),
            vmem(4, 3, 8),
            vmem(3, 2, 4, 8),
            vmem(3, 2, 4, 8),
            pltpu.VMEM((512, 3 * WIDE), BF16),
            pltpu.VMEM((512, 4 * WIDE), F32),
            vmem(4, 2, 16, 2),
            vmem(4, 2, 32, 2),
            vmem(3, 4, 32),
            vmem(3, 4, 32),
            vmem(3, 2, 128),
            dma((6,)),
            dma((3, 2)),
            dma((2,)),
            dma((4,)),
            dma((4,)),
            dma((4,)),
            dma((4,)),
            dma((4, 2)),
            dma((4, 2)),
            dma((4, 2)),
            dma((4, 2)),
            dma((4,)),
            dma((4,)),
        ],
        compiler_params=pltpu.CompilerParams(
            collective_id=0, has_side_effects=True, vmem_limit_bytes=60 * 2**20
        ),
        name="butterfly",
    )(coeffs, phases, field_phases, spread, last)


def complete_kernel(
    done, gz3, gy3, field_phases, w_last, out, held, gzv, gyv, fpv, wf_ref, cos_f, sin_f, xs, res, in_sem, out_sem
):
    pick = (lax.axis_index("qx") // 4) * 2 + lax.axis_index("qy") // 8
    half = held.shape[0] // 2
    first, second = pl.ds(0, half), pl.ds(half, half)
    upper, lower = pl.ds(0, 8), pl.ds(8, 8)
    loads = [
        pltpu.make_async_copy(src, dst, in_sem.at[n])
        for n, (src, dst) in enumerate(
            [(field_phases, fpv), (w_last.at[pick], wf_ref), (gz3, gzv), (gy3, gyv)]
        )
    ]
    finished = [(first, 0), (second, 0), (slice(None), 1, slice(None), upper)]
    into = [
        pltpu.make_async_copy(done.at[part], held.at[part], in_sem.at[4 + n])
        for n, part in enumerate(finished)
    ]
    for copy in loads + into:
        copy.start()
    parts = finished + [(slice(None), 1, k, lower) for k in range(2)]
    onto = [
        pltpu.make_async_copy(held.at[part], out.at[part], out_sem.at[n]) for n, part in enumerate(parts)
    ]

    loads[0].wait()
    field_turns(fpv, cos_f, sin_f)
    loads[1].wait()
    for k, got in enumerate((gzv, gyv)):
        loads[2 + k].wait()

        def put(place, value, k=k):
            held[place, 1, k, 8:16, :] = value

        last_stage(got, put, k, 1, xs, res, wf_ref, cos_f, sin_f)
        onto[3 + k].start()
        if k == 0:
            for n in range(3):
                into[n].wait()
                onto[n].start()
    for copy in onto:
        copy.wait()


def complete(done, gz3, gy3, field_phases, last):
    return pl.pallas_call(
        complete_kernel,
        out_shape=jax.ShapeDtypeStruct(done.shape, F32),
        in_specs=[pl.BlockSpec(memory_space=pltpu.HBM)] * 5,
        out_specs=pl.BlockSpec(memory_space=pltpu.HBM),
        scratch_shapes=[
            pltpu.VMEM(done.shape, F32),
            pltpu.VMEM((4, 32, 8, WIDE), F32),
            pltpu.VMEM((4, 32, 8, WIDE), F32),
            pltpu.VMEM((8, 32, WIDE), F32),
            pltpu.VMEM((3 * WIDE, 2 * WIDE), BF16),
            pltpu.VMEM((2, 8, 32, WIDE), F32),
            pltpu.VMEM((2, 8, 32, WIDE), F32),
            pltpu.VMEM((512, 3 * WIDE), BF16),
            pltpu.VMEM((512, 2 * WIDE), F32),
            pltpu.SemaphoreType.DMA((7,)),
            pltpu.SemaphoreType.DMA((5,)),
        ],
        compiler_params=pltpu.CompilerParams(vmem_limit_bytes=60 * 2**20),
        name="complete",
    )(done, gz3, gy3, field_phases, last)


def per_device(coeffs, level_phase, field_phase):
    spread, last = weights()
    angles = field_phase.reshape(8, 32, WIDE)
    done, gz3, gy3 = butterfly(
        coeffs.reshape(128, 2, 2, 16, WIDE), level_phase.reshape(128, 8, WIDE), angles, spread, last
    )
    return complete(done, gz3, gy3, angles, last).reshape(coeffs.shape)


def solution(mesh):
    return jax.shard_map(
        per_device,
        mesh=mesh,
        in_specs=(
            P("qx", "qy", None, None, None, None, None, None),
            P("qx", "qy", None, None, None, None, None),
            P("qx", "qy", None, None, None, None),
        ),
        out_specs=P("qx", "qy", None, None, None, None, None, None),
        check_vma=False,
    )
```

```python
import functools

import jax
import jax.numpy as jnp
import numpy as np
from jax import lax
from jax.experimental import pallas as pl
from jax.experimental.pallas import tpu as pltpu
from jax.sharding import PartitionSpec as P

CHEB = 8
PTS = CHEB * CHEB
WIDE = 2 * PTS
MESH = pl.DeviceIdType.MESH
F32 = jnp.float32
BF16 = jnp.bfloat16
DIGITS = [(a, b, c) for a in range(2) for b in range(2) for c in range(2)]


def point_tables(count):
    points = 0.5 - 0.5 * np.cos((2 * np.arange(count) + 1) * np.pi / (2 * count))

    def lagrange(places):
        values = np.ones((len(places), count))
        for k in range(count):
            for m in range(count):
                if m != k:
                    values[:, k] = values[:, k] * (places - points[m]) / (points[k] - points[m])
        return values

    halves = [lagrange((q + points) / 2.0) for q in range(2)]
    uniform = lagrange((np.arange(count) + 0.5) / count)
    identity = np.eye(2)
    children = [
        [np.kron(identity, np.kron(halves[q], halves[s])).T for s in range(2)] for q in range(2)
    ]
    evaluate = np.kron(identity, np.kron(uniform, uniform)).T
    return children, evaluate


def three_parts(matrix):
    high = matrix.astype(np.float32).astype(BF16)
    low = (matrix - high.astype(np.float64)).astype(np.float32).astype(BF16)
    return np.concatenate([high, high, low], axis=0)


def weights():
    children, evaluate = point_tables(CHEB)
    spread = three_parts(np.concatenate([children[q][s] for q in range(2) for s in range(2)], axis=1))
    last = []
    for q in range(2):
        for s in range(2):
            both = children[q][s] @ evaluate
            swapped = np.concatenate([both[:, PTS:], both[:, :PTS]], axis=1)
            last.append(three_parts(np.concatenate([both, swapped], axis=1)))
    return jnp.asarray(spread), jnp.asarray(np.stack(last))


def split_parts(value):
    high = value.astype(BF16)
    low = (value - high.astype(F32)).astype(BF16)
    return high, low


def sine_cosine(angle):
    u = angle * 0.5
    w = u * u
    s = -2.5052108e-08
    for c in (2.7557319e-06, -1.9841270e-04, 8.3333333e-03, -1.6666667e-01, 1.0):
        s = s * w + c
    s = s * u
    c_ = 2.0876757e-09
    for c in (-2.7557319e-07, 2.4801587e-05, -1.3888889e-03, 4.1666667e-02, -0.5, 1.0):
        c_ = c_ * w + c
    return 2.0 * s * c_, 1.0 - 2.0 * s * s


def swap(value):
    return pltpu.roll(value, PTS, value.ndim - 1)


def turn_tables(angle, before):
    sine, cosine = sine_cosine(angle)
    lane = lax.broadcasted_iota(jnp.int32, angle.shape, angle.ndim - 1)
    low = lane < PTS
    cos_swap, sin_swap = swap(cosine), swap(sine)
    cos = (jnp.where(low, cosine, cos_swap), jnp.where(low, cos_swap, cosine))
    if before:
        sin = (jnp.where(low, sine, -sin_swap), jnp.where(low, sin_swap, -sine))
    else:
        sin = (jnp.where(low, -sine, sin_swap), jnp.where(low, -sin_swap, sine))
    return cos, sin


def place_parts(xs, row, value):
    high, low = split_parts(value)
    rows = pl.ds(pl.multiple_of(row, 16), 16)
    xs[rows, 0:WIDE] = high
    xs[rows, WIDE : 2 * WIDE] = low
    xs[rows, 2 * WIDE : 3 * WIDE] = high


def last_stage(got, put, k, left, xs, res, wf_ref, cos_f, sin_f):
    def piece(p, carry):
        for a in range(2):
            for n in range(16):
                place_parts(xs, (a * 16 + n) * 16, got[p * 2 + a, pl.ds(2 * n, 2)].reshape(16, WIDE))
        res[:, 0 : 2 * WIDE] = jnp.dot(xs[...], wf_ref[...], preferred_element_type=F32)
        for a in range(2):
            for n in range(32):
                if k == 0:
                    box_h, box_v = p * 4 + (a * 2 + n // 16), n % 16
                else:
                    box_h, box_v = n // 4, p * 8 + (a * 4 + n % 4)
                rows = slice((a * 32 + n) * 8, (a * 32 + n + 1) * 8)
                at = pl.ds(box_v * 2 + left, 1)
                put(
                    box_h * 16 + box_v,
                    res[rows, 0:WIDE] * cos_f[k, box_h, at, :]
                    + res[rows, WIDE : 2 * WIDE] * sin_f[k, box_h, at, :],
                )
        return carry

    lax.fori_loop(0, 2, piece, 0)


def field_turns(fpv, cos_f, sin_f):
    def table(i, carry):
        cos, sin = turn_tables(fpv[i], False)
        for k in range(2):
            cos_f[k, i] = cos[k]
            sin_f[k, i] = sin[k]
        return carry

    lax.fori_loop(0, 8, table, 0)


def wait_for(ref, sem):
    pltpu.make_async_copy(ref, ref, sem).wait()


def butterfly_kernel(
    coeffs, phases, field_phases, w_all, w_last, out, gz3, gy3,
    cbuf, lpv, fpv, w_ref, wf_ref, cos1, sin1, cos_f, sin_f,
    send_a, recv_xa, send_ya, recv_ya, send_yb, recv_yb, recv_xb,
    pk, p1, pq, phs, cos_t, sin_t, xs, res, s4, r1, gz, gy, done,
    load_sem, out_sem, own_sem, x_send, x_recv, in_send, in_recv, s1_send, s1_recv, s2_send, s2_recv, ph_send, ph_recv,
):
    big_x = lax.axis_index("qx")
    big_y = lax.axis_index("qy")
    z, core = big_x // 2, big_x % 2
    y, x = big_y // 4, big_y % 4
    pick = (z // 2) * 2 + y // 2

    loads = [
        pltpu.make_async_copy(src, dst, load_sem.at[n])
        for n, (src, dst) in enumerate(
            [
                (phases, lpv),
                (coeffs.at[:, 0], cbuf.at[0]),
                (coeffs.at[:, 1], cbuf.at[1]),
                (w_all, w_ref),
                (field_phases, fpv),
                (w_last.at[pick], wf_ref),
            ]
        )
    ]
    for load in loads:
        load.start()

    zs = [(z + d) % 4 for d in range(4)]
    cs = [core, 1 - core]
    ys = [(y + d) % 4 for d in range(4)]
    xs_ = [(x + d) % 4 for d in range(4)]
    y_odd = [(y + d) % 2 for d in range(4)]
    z_odd = [(z + d) % 2 for d in range(4)]
    dev_x = [[zs[dz] * 2 + cs[dc] for dc in range(2)] for dz in range(4)]
    dev_y = [[ys[dy] * 4 + xs_[dx] for dx in range(4)] for dy in range(4)]

    barrier = pltpu.get_barrier_semaphore()
    greeted = 0
    for dz in range(4):
        for dc in range(2):
            for dy in range(4):
                for dx in range(4):
                    if (dz, dc, dy, dx) != (0, 0, 0, 0) and 0 in (dz, dy, dx):
                        pl.semaphore_signal(
                            barrier, inc=1, device_id=(dev_x[dz][dc], dev_y[dy][dx]), device_id_type=MESH
                        )
                        greeted += 1

    def send(src, dst, send_sem, recv_sem, target):
        pltpu.make_async_remote_copy(
            src_ref=src, dst_ref=dst, send_sem=send_sem, recv_sem=recv_sem,
            device_id=target, device_id_type=MESH,
        ).start()

    me_in = big_x * 4 + y
    me_z = core * 16 + y * 4 + x
    me_y = big_x * 4 + x

    loads[0].wait()

    def first_tables(i, carry):
        some = pl.ds(i * 8, 8)
        cos, sin = turn_tables(lpv[some], True)
        for k in range(2):
            cos1[k, some] = cos[k]
            sin1[k, some] = sin[k]
        return carry

    lax.fori_loop(0, 16, first_tables, 0)

    def rotate_first(c):
        left, half = c // 2, c % 2
        if half == 0:
            loads[1 + left].wait()

        def step(j, carry):
            for n in range(16):
                i = j * 4 + n // 4
                vx = n % 4
                box = j * 16 + n
                direct = None
                crossed = None
                for k in range(2):
                    value = cbuf[left, box, k, pl.ds(half * 8, 8), :]
                    d = value * cos1[k, box, pl.ds(left, 1), :]
                    e = value * sin1[k, box, pl.ds(left, 1), :]
                    direct = d if direct is None else direct + d
                    crossed = e if crossed is None else crossed + e
                if left == 0:
                    send_a[half, vx, i] = direct + swap(crossed)
                else:
                    send_yb[half, i, vx] = direct + swap(crossed)
            return carry

        lax.fori_loop(0, 8, step, 0)

    def send_x(src, dst, send_sem, recv_sem):
        for dx in range(1, 4):
            send(src(xs_[dx]), dst, send_sem, recv_sem, (big_x, dev_y[0][dx]))

    def send_in(src, dst, send_sem, recv_sem):
        for d in range(31, 0, -1):
            there_x = dev_x[d // 8][(d // 4) % 2]
            send(src(there_x * 4 + ys[d % 4]), dst, send_sem, recv_sem, (there_x, dev_y[d % 4][0]))

    def enter(c):
        h = c % 2
        if c < 2:
            send_x(lambda t: send_a.at[h, t], recv_xa.at[h, x], x_send.at[c], x_recv.at[c])
        else:
            send_in(lambda t: send_yb.at[h, t], recv_yb.at[h, me_in], in_send.at[c], in_recv.at[c])

    def pass_on(c):
        h = c % 2
        if c < 2:
            wait_for(recv_xa.at[h, pl.ds(0, 3)], x_recv.at[c])
            recv_xa[h, x] = send_a[h, x]

            def add(j, carry):
                some = pl.ds(j * 8, 8)
                for y1 in range(2):
                    send_ya[h, some, y1] = recv_xa[h, 2 * y1, some] + recv_xa[h, 2 * y1 + 1, some]
                return carry

            lax.fori_loop(0, 4, add, 0)
            send_in(lambda t: send_ya.at[h, t], recv_ya.at[h, me_in], in_send.at[c], in_recv.at[c])
            recv_ya[h, me_in] = send_ya[h, me_in]
        else:
            wait_for(recv_yb.at[h, pl.ds(0, 31)], in_recv.at[c])
            recv_yb[h, me_in] = send_yb[h, me_in]
            send_x(lambda t: recv_yb.at[h, :, t], recv_xb.at[h, x], x_send.at[c], x_recv.at[c])
            recv_xb[h, x] = recv_yb[h, :, x]

    spans = (pl.ds(0, 1), pl.ds(1, 2))

    def pack_phases(j, carry):
        for n in range(4):
            i = j * 4 + n
            for level in range(3):
                for vx in range(4):
                    pk[i, level, 2 * vx : 2 * vx + 2] = lpv[i * 4 + vx, 2 * level + 2 : 2 * level + 4]
        return carry

    def send_phases(part):
        span = spans[part]
        send_in(lambda t: pk.at[t, span], p1.at[me_in, span], ph_send.at[part], ph_recv.at[part])
        p1[me_in, span] = pk[me_in, span]

    def pass_phases(part):
        span = spans[part]
        wait_for(p1.at[pl.ds(0, 31), span], ph_recv.at[part])

        def pack(i, carry):
            for level in (0,) if part == 0 else (1, 2):
                for sx in range(4):
                    for sy in range(4):
                        pq[sx, level, i, 2 * sy : 2 * sy + 2] = p1[i * 4 + sy, level, 2 * sx : 2 * sx + 2]
            return carry

        lax.fori_loop(0, 8, pack, 0)
        send_x(lambda t: pq.at[t, span], phs.at[x, span], ph_send.at[2 + part], ph_recv.at[2 + part])
        phs[x, span] = pq[x, span]

    def phase_tables(part):
        span = spans[part]
        wait_for(phs.at[pl.ds(0, 3), span], ph_recv.at[2 + part])

        def table(sx, carry):
            for level in (0,) if part == 0 else (1, 2):
                cos, sin = turn_tables(phs[sx, level], True)
                for k in range(2):
                    cos_t[level, k, sx] = cos[k]
                    sin_t[level, k, sx] = sin[k]
            return carry

        lax.fori_loop(0, 4, table, 0)

    def field_tables():
        loads[4].wait()
        field_turns(fpv, cos_f, sin_f)

    def put_parts(row, value):
        place_parts(xs, row, value)

    def multiply():
        res[...] = jnp.dot(xs[...], w_ref[...], preferred_element_type=F32)

    def turned_sum(parts, level, left):
        direct = None
        crossed = None
        for block, column, k, at_x, at_y, at_v in parts:
            value = res[pl.ds(pl.multiple_of(block * 8, 8), 8), column * WIDE : (column + 1) * WIDE]
            row = pl.ds(2 * at_y + left, 1)
            d = value * cos_t[level, k, at_v, at_x, row, :]
            e = value * sin_t[level, k, at_v, at_x, row, :]
            direct = d if direct is None else direct + d
            crossed = e if crossed is None else crossed + e
        return direct + swap(crossed)

    def level_one(c):
        h = c % 2
        if c < 2:
            wait_for(recv_ya.at[h, pl.ds(0, 31)], in_recv.at[c])
        else:
            wait_for(recv_xb.at[h, pl.ds(0, 3)], x_recv.at[c])

        def first(j, carry):
            for n in range(8):
                i = j * 8 + n
                if c < 2:
                    value = recv_ya[h, i].reshape(16, WIDE)
                else:
                    value = jnp.concatenate(
                        [recv_xb[h, 2 * y1, i] + recv_xb[h, 2 * y1 + 1, i] for y1 in range(2)], axis=0
                    )
                put_parts(i * 16, value)
            return carry

        lax.fori_loop(0, 4, first, 0)
        multiply()

    def level_two(c):
        left = c // 2

        def second(a, carry):
            for y3, y2, y0 in DIGITS:
                outs = []
                for k in range(2):
                    parts = []
                    for x0 in range(2):
                        for y1 in range(2):
                            block = a * 16 + (x0 * 8 + y3 * 4 + y2 * 2 + y1)
                            parts.append((block, k * 2 + y0, k, a * 2 + x0, y3 * 2 + y2, y1 * 2 + y0))
                    outs.append(turned_sum(parts, 0, left))
                put_parts(a * 128 + (y3 * 4 + y2 * 2 + y0) * 16, jnp.concatenate(outs, axis=0))
            return carry

        lax.fori_loop(0, 4, second, 0)
        multiply()

    def other_levels(c):
        left = c // 2

        def third(x2, carry):
            for y3, y0, k in DIGITS:
                for x0 in range(2):
                    outs = []
                    for y1 in range(2):
                        parts = []
                        for x1 in range(2):
                            for y2 in range(2):
                                block = x2 * 32 + (x1 * 16 + y3 * 8 + y2 * 4 + y0 * 2 + k)
                                at_x = x2 * 4 + (x1 * 2 + x0)
                                parts.append((block, x0 * 2 + y1, k, at_x, y3 * 2 + y2, y1 * 2 + y0))
                        outs.append(turned_sum(parts, 1, left))
                    put_parts(
                        x2 * 256 + (y3 * 8 + y0 * 4 + k * 2 + x0) * 16, jnp.concatenate(outs, axis=0)
                    )
            return carry

        lax.fori_loop(0, 2, third, 0)
        multiply()

        def fourth(y0, carry):
            for k, x0, y1 in DIGITS:
                for x1 in range(2):
                    for y2 in range(2):
                        parts = []
                        for x2 in range(2):
                            for y3 in range(2):
                                block = y0 * 8 + (x2 * 32 + y3 * 16 + k * 4 + x0 * 2 + y1)
                                at_x = x2 * 4 + x1 * 2 + x0
                                parts.append((block, x1 * 2 + y2, k, at_x, y3 * 2 + y2, y1 * 2 + y0))
                        if k == 0:
                            s4[c, 0, y0 + (x0 * 8 + y2 * 4 + y1 * 2), x1] = turned_sum(parts, 2, left)
                        else:
                            s4[c, 1, y0 + (x1 * 8 + x0 * 4 + y1 * 2), y2] = turned_sum(parts, 2, left)
            return carry

        lax.fori_loop(0, 2, fourth, 0)

        for d in range(31, 0, -1):
            dc, dt, dx = d // 16, (d // 4) % 4, d % 4
            send(
                s4.at[c, 0, cs[dc] * 8 + y_odd[dt] * 4 + xs_[dx]], r1.at[c, 0, me_z],
                s1_send.at[c, 0], s1_recv.at[c, 0], (dev_x[0][dc], dev_y[dt][dx]),
            )
            send(
                s4.at[c, 1, z_odd[dt] * 8 + cs[dc] * 4 + xs_[dx]], r1.at[c, 1, me_y],
                s1_send.at[c, 1], s1_recv.at[c, 1], (dev_x[dt][dc], dev_y[0][dx]),
            )
        r1[c, 0, me_z] = s4[c, 0, core * 8 + y_odd[0] * 4 + x]
        r1[c, 1, me_y] = s4[c, 1, z_odd[0] * 8 + core * 4 + x]

    def out_last(c, k):
        wait_for(r1.at[c, k, pl.ds(0, 31)], s1_recv.at[c, k])
        to_z, to_y = (gz3, gy3) if c == 3 else (gz.at[c], gy.at[c])
        for d in (1, 3, 2):
            if k == 0:
                send(
                    r1.at[c, 0, :, z_odd[d]], to_z.at[z], s2_send.at[c, 0], s2_recv.at[c, 0],
                    (dev_x[d][0], big_y),
                )
            else:
                send(
                    r1.at[c, 1, :, y_odd[d]], to_y.at[y], s2_send.at[c, 1], s2_recv.at[c, 1],
                    (big_x, dev_y[d][0]),
                )
        if c == 3:
            kept.append(
                pltpu.make_async_copy(r1.at[c, 0, :, z_odd[0]], gz3.at[z], own_sem.at[0])
                if k == 0
                else pltpu.make_async_copy(r1.at[c, 1, :, y_odd[0]], gy3.at[y], own_sem.at[1])
            )
            kept[-1].start()
        elif k == 0:
            gz[c, z] = r1[c, 0, :, z_odd[0]]
        else:
            gy[c, y] = r1[c, 1, :, y_odd[0]]

    def finish(c, k):
        left, half = c // 2, c % 2
        got = gz if k == 0 else gy
        wait_for(got.at[c, pl.ds(0, 3)], s2_recv.at[c, k])

        def put(place, value):
            done[c, k, place] = value

        last_stage(got.at[c], put, k, left, xs, res, wf_ref, cos_f, sin_f)
        store = pltpu.make_async_copy(
            done.at[c, k], out.at[:, left, k, pl.ds(half * 8, 8)], out_sem.at[c, k]
        )
        store.start()
        stores.append(store)

    stores = []
    kept = []
    lax.fori_loop(0, 8, pack_phases, 0)
    rotate_first(0)
    pl.semaphore_wait(barrier, greeted)
    enter(0)
    send_phases(0)
    send_phases(1)
    rotate_first(2)
    enter(2)
    rotate_first(1)
    enter(1)
    pass_phases(0)
    pass_phases(1)
    pass_on(0)
    pass_on(2)
    pass_on(1)
    rotate_first(3)
    enter(3)
    loads[3].wait()
    field_tables()
    level_one(0)
    phase_tables(0)
    level_two(0)
    phase_tables(1)
    other_levels(0)
    level_one(1)
    level_two(1)
    other_levels(1)
    out_last(0, 0)
    pass_on(3)
    level_one(2)
    out_last(0, 1)
    out_last(1, 0)
    out_last(1, 1)
    level_two(2)
    other_levels(2)
    level_one(3)
    level_two(3)
    other_levels(3)
    out_last(2, 0)
    out_last(2, 1)
    loads[5].wait()
    finish(0, 0)
    out_last(3, 1)
    finish(1, 0)
    out_last(3, 0)
    finish(0, 1)
    finish(1, 1)
    finish(2, 0)
    finish(2, 1)
    wait_for(gz3.at[pl.ds(0, 3)], s2_recv.at[3, 0])
    wait_for(gy3.at[pl.ds(0, 3)], s2_recv.at[3, 1])
    for c in range(4):
        h = c % 2
        wait_for(recv_xa.at[h, pl.ds(0, 3)], x_send.at[c])
        wait_for((recv_ya if c < 2 else recv_yb).at[h, pl.ds(0, 31)], in_send.at[c])
        for k in range(2):
            wait_for(r1.at[c, k, pl.ds(0, 31)], s1_send.at[c, k])
            wait_for(gz.at[0, pl.ds(0, 3)], s2_send.at[c, k])
    for store in stores + kept:
        store.wait()
    for part in range(2):
        wait_for(p1.at[pl.ds(0, 31), spans[part]], ph_send.at[part])
        wait_for(phs.at[pl.ds(0, 3), spans[part]], ph_send.at[2 + part])


def butterfly(coeffs, phases, field_phases, spread, last):
    dma = pltpu.SemaphoreType.DMA
    tile = (8, WIDE)

    def vmem(*shape):
        return pltpu.VMEM(shape + tile, F32)

    return pl.pallas_call(
        butterfly_kernel,
        out_shape=(
            jax.ShapeDtypeStruct((128, 2, 2, 16, WIDE), F32),
            jax.ShapeDtypeStruct((4, 32) + tile, F32),
            jax.ShapeDtypeStruct((4, 32) + tile, F32),
        ),
        in_specs=[pl.BlockSpec(memory_space=pltpu.HBM)] * 5,
        out_specs=tuple(pl.BlockSpec(memory_space=pltpu.HBM) for _ in range(3)),
        scratch_shapes=[
            pltpu.VMEM((2, 128, 2, 16, WIDE), F32),
            vmem(128),
            pltpu.VMEM((8, 32, WIDE), F32),
            pltpu.VMEM((3 * WIDE, 4 * WIDE), BF16),
            pltpu.VMEM((3 * WIDE, 2 * WIDE), BF16),
            vmem(2, 128),
            vmem(2, 128),
            pltpu.VMEM((2, 8, 32, WIDE), F32),
            pltpu.VMEM((2, 8, 32, WIDE), F32),
            vmem(2, 4, 32),
            vmem(2, 4, 32),
            vmem(2, 32, 2),
            vmem(2, 32, 2),
            vmem(2, 32, 4),
            vmem(2, 32, 4),
            vmem(2, 4, 32),
            vmem(32, 3),
            vmem(32, 3),
            vmem(4, 3, 8),
            vmem(4, 3, 8),
            vmem(3, 2, 4, 8),
            vmem(3, 2, 4, 8),
            pltpu.VMEM((512, 3 * WIDE), BF16),
            pltpu.VMEM((512, 4 * WIDE), F32),
            vmem(4, 2, 16, 2),
            vmem(4, 2, 32, 2),
            vmem(3, 4, 32),
            vmem(3, 4, 32),
            vmem(3, 2, 128),
            dma((6,)),
            dma((3, 2)),
            dma((2,)),
            dma((4,)),
            dma((4,)),
            dma((4,)),
            dma((4,)),
            dma((4, 2)),
            dma((4, 2)),
            dma((4, 2)),
            dma((4, 2)),
            dma((4,)),
            dma((4,)),
        ],
        compiler_params=pltpu.CompilerParams(
            collective_id=0, has_side_effects=True, vmem_limit_bytes=60 * 2**20
        ),
        name="butterfly",
    )(coeffs, phases, field_phases, spread, last)


def complete_kernel(
    done, gz3, gy3, field_phases, w_last, out, held, gzv, gyv, fpv, wf_ref, cos_f, sin_f, xs, res, in_sem, out_sem
):
    pick = (lax.axis_index("qx") // 4) * 2 + lax.axis_index("qy") // 8
    half = held.shape[0] // 2
    first, second = pl.ds(0, half), pl.ds(half, half)
    upper, lower = pl.ds(0, 8), pl.ds(8, 8)
    loads = [
        pltpu.make_async_copy(src, dst, in_sem.at[n])
        for n, (src, dst) in enumerate(
            [(field_phases, fpv), (w_last.at[pick], wf_ref), (gz3, gzv), (gy3, gyv)]
        )
    ]
    finished = [(first, 0), (second, 0), (slice(None), 1, slice(None), upper)]
    into = [
        pltpu.make_async_copy(done.at[part], held.at[part], in_sem.at[4 + n])
        for n, part in enumerate(finished)
    ]
    for copy in loads + into:
        copy.start()
    parts = finished + [(slice(None), 1, k, lower) for k in range(2)]
    onto = [
        pltpu.make_async_copy(held.at[part], out.at[part], out_sem.at[n]) for n, part in enumerate(parts)
    ]

    loads[0].wait()
    field_turns(fpv, cos_f, sin_f)
    loads[1].wait()
    for k, got in enumerate((gzv, gyv)):
        loads[2 + k].wait()

        def put(place, value, k=k):
            held[place, 1, k, 8:16, :] = value

        last_stage(got, put, k, 1, xs, res, wf_ref, cos_f, sin_f)
        onto[3 + k].start()
        if k == 0:
            for n in range(3):
                into[n].wait()
                onto[n].start()
    for copy in onto:
        copy.wait()


def complete(done, gz3, gy3, field_phases, last):
    return pl.pallas_call(
        complete_kernel,
        out_shape=jax.ShapeDtypeStruct(done.shape, F32),
        in_specs=[pl.BlockSpec(memory_space=pltpu.HBM)] * 5,
        out_specs=pl.BlockSpec(memory_space=pltpu.HBM),
        scratch_shapes=[
            pltpu.VMEM(done.shape, F32),
            pltpu.VMEM((4, 32, 8, WIDE), F32),
            pltpu.VMEM((4, 32, 8, WIDE), F32),
            pltpu.VMEM((8, 32, WIDE), F32),
            pltpu.VMEM((3 * WIDE, 2 * WIDE), BF16),
            pltpu.VMEM((2, 8, 32, WIDE), F32),
            pltpu.VMEM((2, 8, 32, WIDE), F32),
            pltpu.VMEM((512, 3 * WIDE), BF16),
            pltpu.VMEM((512, 2 * WIDE), F32),
            pltpu.SemaphoreType.DMA((7,)),
            pltpu.SemaphoreType.DMA((5,)),
        ],
        compiler_params=pltpu.CompilerParams(vmem_limit_bytes=60 * 2**20),
        name="complete",
    )(done, gz3, gy3, field_phases, last)


def per_device(coeffs, level_phase, field_phase):
    spread, last = weights()
    angles = field_phase.reshape(8, 32, WIDE)
    done, gz3, gy3 = butterfly(
        coeffs.reshape(128, 2, 2, 16, WIDE), level_phase.reshape(128, 8, WIDE), angles, spread, last
    )
    return complete(done, gz3, gy3, angles, last).reshape(coeffs.shape)


def solution(mesh):
    return jax.shard_map(
        per_device,
        mesh=mesh,
        in_specs=(
            P("qx", "qy", None, None, None, None, None, None),
            P("qx", "qy", None, None, None, None, None),
            P("qx", "qy", None, None, None, None),
        ),
        out_specs=P("qx", "qy", None, None, None, None, None, None),
        check_vma=False,
    )
```
